128 devices in a mesh: dp: 32 (over z, x, core), sect: 4 (over y).
Axes of the slice: x: 4, y: 4, z: 4, core: 2. Of those that a mesh axis runs over, the one named last changes fastest.
Arguments:
- queries: bfloat16 [32, 16, 8192], P('dp', None, 'sect'), may hold values from -5 to 5
- keys: bfloat16 [32, 16, 8192], P('dp', None, 'sect'), may hold values from -5 to 5
- values: bfloat16 [32, 16, 8192], P('dp', None, 'sect'), may hold values from -6 to 6
- residual: bfloat16 [32, 16, 8192], P('dp'), may hold values from -6 to 6
- labels: int32 [32, 16], P('dp'), may hold values from 0 to 2, as said below
- slot_modality: int32 [4], replicated, may hold values from 0 to 2, as said below
- gains: float32 [3, 8192], replicated, may hold values from 0.1 to 1.9
- up_weight: bfloat16 [4, 11008, 8192], P('sect', 'dp'), may hold values from -0.0625 to 0.0625
- down_weight: bfloat16 [4, 11008, 8192], P('sect', 'dp'), may hold values from -0.0546875 to 0.0546875
- cotangent: bfloat16 [32, 16, 8192], P('dp'), may hold values from -6 to 6
Outputs:
- output: bfloat16 [32, 16, 8192], P('dp', 'sect')
- residual_grad: bfloat16 [32, 16, 8192], P('dp', 'sect')
- query_grad: bfloat16 [32, 16, 8192], P('dp', None, 'sect')
- key_grad: bfloat16 [32, 16, 8192], P('dp', None, 'sect')
- value_grad: bfloat16 [32, 16, 8192], P('dp', None, 'sect')
- up_grad: bfloat16 [4, 11008, 8192], P('sect', 'dp')
- down_grad: bfloat16 [4, 11008, 8192], P('sect', 'dp')
- gain_grad: float32 [3, 8192], replicated
The draws below stay inside these ranges and needn't reach their ends.
Inputs may be any that keep to these rules, and one draw needn't show every extreme that they name: `labels`: every sequence holds exactly 8 text tokens (label 0); its other tokens are image or speech. `slot_modality`: text owns two slots, image one, speech one.
All inputs are finite; a program needn't handle non-finite values.
Results may differ from the reference program's by a relative error of at most 0.015.
The reference program's roundings to bfloat16 on the way count: a program that leaves them out, or rounds other values in their place, can miss the bound.
Values may be sent and summed in bfloat16 or wider, within the bound.
No kernel may reach another device: no remote copies, remote signals or barrier semaphores. Data moves between devices by JAX's collectives and lax.ppermute only.
A program may use at most 128 MiB of HBM per device.

```python
import jax
import jax.numpy as jnp
from jax import lax

D = 8192
HD = 128
FH = 11008
MODALITIES = 3
L = 16
SEQS = 32
N_SECT = 4


def attention_pair(key):
    base_key = jax.random.fold_in(key, 7)
    first, second = jax.random.split(base_key, 2)
    shape = (SEQS, L, D)
    key_vals = jnp.clip(jax.random.normal(first, shape, jnp.float32), -5.0, 5.0)
    query_vals = jnp.clip(jax.random.normal(second, shape, jnp.float32), -5.0, 5.0)
    return (query_vals, key_vals)


def draw_queries(key, part):
    return attention_pair(key)[0].astype(jnp.bfloat16)


def draw_keys(key, part):
    return attention_pair(key)[1].astype(jnp.bfloat16)


def draw_labels(key, part):
    seq_keys = jax.random.split(jax.random.fold_in(key, 3), SEQS)
    orders = jax.vmap(lambda one_key: jax.random.permutation(one_key, L))(seq_keys)
    others = jax.random.randint(jax.random.fold_in(key, 5), (SEQS, L), 1, 3)
    return jnp.where(orders < L // 2, 0, others).astype(jnp.int32)


def draw_slot_modality(key, part):
    order = jax.random.permutation(jax.random.fold_in(key, 9), 4)
    table = jnp.array([0, 0, 1, 2], jnp.int32)
    return jnp.take(table, order).astype(jnp.int32)


def block_levels(own_key, shape, pieces, smallest, high):
    loudness, own = 1.0, jax.random.fold_in(own_key, 6)
    for dim, parts in pieces:
        draws = jnp.exp(jax.random.uniform(jax.random.fold_in(own, dim), (parts,), jnp.float32, smallest / len(pieces), high / len(pieces)))
        loudness = loudness * jnp.repeat(draws, shape[dim] // parts).reshape([-1 if axis == dim else 1 for axis in range(len(shape))])
    return loudness


def centred(key, dims, deviation, bound, pieces=(), dtype=jnp.bfloat16):
    values = deviation * jax.random.normal(key, dims, jnp.float32)
    if pieces:
        values = values * block_levels(key, dims, pieces, -0.22, 0.18)
    return jnp.clip(values, -bound, bound).astype(dtype)


def setup_inputs(seed: int = 0) -> dict:
    key_of = jax.random.split(jax.random.key(seed), 11)
    queries = draw_queries(jax.random.fold_in(key_of[10], 71), 0)
    keys = draw_keys(jax.random.fold_in(key_of[10], 71), 0)
    values = centred(key_of[2], (SEQS, L, D), 1.0, 6.0, ((0, 32), (2, 4)))
    residual = centred(key_of[3], (SEQS, L, D), 1.0, 6.0, ((0, 32),))
    labels = draw_labels(jax.random.fold_in(key_of[10], 71), 0)
    slot_modality = draw_slot_modality(jax.random.fold_in(key_of[10], 71), 0)
    gains = jnp.clip(1.0 + 0.18 * jax.random.normal(key_of[6], (MODALITIES, D), jnp.float32), 0.1, 1.9)
    up_weight = centred(key_of[7], (N_SECT, FH, D), D ** -0.5, 0.0625, ((0, 4), (1, 32)))
    down_weight = centred(key_of[8], (N_SECT, FH, D), FH ** -0.5, 0.0546875, ((0, 4), (1, 32)))
    cotangent = centred(key_of[9], (SEQS, L, D), 1.0, 6.0, ((0, 32),))
    return {"queries": queries, "keys": keys, "values": values, "residual": residual, "labels": labels, "slot_modality": slot_modality, "gains": gains, "up_weight": up_weight, "down_weight": down_weight, "cotangent": cotangent}


def causal_forward(queries, keys, values):
    seq_count, length, width = queries.shape
    head_count = width // HD
    query_f = queries.astype(jnp.float32).reshape(seq_count, length, head_count, HD)
    key_f = keys.astype(jnp.float32).reshape(seq_count, length, head_count, HD)
    value_f = values.astype(jnp.float32).reshape(seq_count, length, head_count, HD)
    scores = jnp.einsum('sqhd,skhd->shqk', query_f, key_f) * HD ** (-0.5)
    position = jnp.arange(length)
    causal = position[:, None] >= position[None, :]
    scores = jnp.where(causal, scores, -1e+30)
    probs = jax.nn.softmax(scores, axis=-1)
    probs_b = probs.astype(jnp.bfloat16)
    attended = jnp.einsum('shqk,skhd->sqhd', probs_b.astype(jnp.float32), value_f)
    return (attended.astype(jnp.bfloat16).reshape(seq_count, length, width), probs, probs_b)

def causal_backward(grad_out, queries, keys, values, attended, probs, probs_b):
    seq_count, length, width = queries.shape
    head_count = width // HD
    shape = (seq_count, length, head_count, HD)
    grad_f = grad_out.astype(jnp.float32).reshape(shape)
    query_f = queries.astype(jnp.float32).reshape(shape)
    key_f = keys.astype(jnp.float32).reshape(shape)
    value_f = values.astype(jnp.float32).reshape(shape)
    attended_f = attended.astype(jnp.float32).reshape(shape)
    value_grad = jnp.einsum('shqk,sqhd->skhd', probs_b.astype(jnp.float32), grad_f).astype(jnp.bfloat16)
    dprob = jnp.einsum('sqhd,skhd->shqk', grad_f, value_f)
    delta = jnp.einsum('sqhd,sqhd->shq', grad_f, attended_f)
    dscore = (probs * (dprob - delta[..., None]) * HD ** (-0.5)).astype(jnp.bfloat16).astype(jnp.float32)
    query_grad = jnp.einsum('shqk,skhd->sqhd', dscore, key_f).astype(jnp.bfloat16)
    key_grad = jnp.einsum('shqk,sqhd->skhd', dscore, query_f).astype(jnp.bfloat16)
    return (query_grad.reshape(seq_count, length, width), key_grad.reshape(seq_count, length, width), value_grad.reshape(seq_count, length, width))

def block_sum(left, weight):
    return jnp.dot(left, weight, preferred_element_type=jnp.float32)

def reference(queries, keys, values, residual, labels, slot_modality, gains, up_weight, down_weight, cotangent):
    attended, probs, probs_b = causal_forward(queries, keys, values)
    hidden = (residual.astype(jnp.float32) + attended.astype(jnp.float32)).astype(jnp.bfloat16)
    hidden_f = hidden.astype(jnp.float32).reshape(-1, D)
    token_labels = labels.reshape(-1)
    onehot = (token_labels[:, None] == jnp.arange(MODALITIES)[None, :]).astype(jnp.float32)
    gain_rows = gains[token_labels]
    inverse = lax.rsqrt(lax.optimization_barrier(jnp.mean(hidden_f * hidden_f, axis=-1, keepdims=True)) + 1e-05)
    normed_f = hidden_f * inverse
    normed = (normed_f * gain_rows).astype(jnp.bfloat16)
    grad_rows = cotangent.reshape(-1, D)
    ffn = jnp.zeros(hidden_f.shape, jnp.float32)
    norm_grad = jnp.zeros(hidden_f.shape, jnp.float32)
    up_grads = []
    down_grads = []
    for slot_number in range(N_SECT):
        keep_mask = (token_labels == slot_modality[slot_number])[:, None]
        slot_rows = jnp.where(keep_mask, normed, jnp.zeros((), jnp.bfloat16))
        slot_cot = jnp.where(keep_mask, grad_rows, jnp.zeros((), jnp.bfloat16))
        preact = jnp.dot(slot_rows, up_weight[slot_number].T, preferred_element_type=jnp.float32)
        activated = jax.nn.silu(preact).astype(jnp.bfloat16)
        ffn = ffn + block_sum(activated, down_weight[slot_number])
        back = jnp.dot(slot_cot, down_weight[slot_number].T, preferred_element_type=jnp.float32)
        sigma = jax.nn.sigmoid(preact)
        pre_grad = (back * sigma * (1.0 + preact * (1.0 - sigma))).astype(jnp.bfloat16)
        down_grads.append(jnp.dot(activated.T, slot_cot, preferred_element_type=jnp.float32).astype(jnp.bfloat16))
        up_grads.append(jnp.dot(pre_grad.T, slot_rows, preferred_element_type=jnp.float32).astype(jnp.bfloat16))
        norm_grad = norm_grad + block_sum(pre_grad, up_weight[slot_number])
    output = (hidden_f + ffn).astype(jnp.bfloat16).reshape(residual.shape)
    scaled = norm_grad * gain_rows
    hidden_grad = grad_rows.astype(jnp.float32) + inverse * (scaled - normed_f * lax.optimization_barrier(jnp.mean(scaled * normed_f, axis=-1, keepdims=True)))
    residual_grad = hidden_grad.astype(jnp.bfloat16).reshape(residual.shape)
    gain_grad = jnp.dot(onehot.T, norm_grad * normed_f, precision=lax.Precision.HIGHEST)
    query_grad, key_grad, value_grad = causal_backward(residual_grad, queries, keys, values, attended, probs, probs_b)
    return (output, residual_grad, query_grad, key_grad, value_grad, jnp.stack(up_grads), jnp.stack(down_grads), gain_grad)
```

```python
import functools

import jax
import jax.numpy as jnp
from jax import lax
from jax.experimental import pallas as pl
from jax.experimental.pallas import tpu as pltpu
from jax.sharding import PartitionSpec as P

HD = 128
MODALITIES = 3
NZ = 4
NX = 4
NC = 2
NS = 4
AXES = ("dp", "sect")
BF = jnp.bfloat16
F32 = jnp.float32
CAP = 8
VMEM = 48 * 1024 * 1024


def causal_forward(queries, keys, values):
    seq_count, length, width = queries.shape
    head_count = width // HD
    query_f = queries.astype(F32).reshape(seq_count, length, head_count, HD)
    key_f = keys.astype(F32).reshape(seq_count, length, head_count, HD)
    value_f = values.astype(F32).reshape(seq_count, length, head_count, HD)
    scores = jnp.einsum("sqhd,skhd->shqk", query_f, key_f) * HD ** (-0.5)
    position = jnp.arange(length)
    causal = position[:, None] >= position[None, :]
    scores = jnp.where(causal, scores, -1e30)
    probs = jax.nn.softmax(scores, axis=-1)
    probs_b = probs.astype(BF)
    attended = jnp.einsum("shqk,skhd->sqhd", probs_b.astype(F32), value_f)
    return (attended.astype(BF).reshape(seq_count, length, width), probs, probs_b)


def causal_backward(grad_out, queries, keys, values, attended, probs, probs_b):
    seq_count, length, width = queries.shape
    head_count = width // HD
    shape = (seq_count, length, head_count, HD)
    grad_f = grad_out.astype(F32).reshape(shape)
    query_f = queries.astype(F32).reshape(shape)
    key_f = keys.astype(F32).reshape(shape)
    value_f = values.astype(F32).reshape(shape)
    attended_f = attended.astype(F32).reshape(shape)
    value_grad = jnp.einsum("shqk,sqhd->skhd", probs_b.astype(F32), grad_f).astype(BF)
    dprob = jnp.einsum("sqhd,skhd->shqk", grad_f, value_f)
    delta = jnp.einsum("sqhd,sqhd->shq", grad_f, attended_f)
    dscore = (probs * (dprob - delta[..., None]) * HD ** (-0.5)).astype(BF).astype(F32)
    query_grad = jnp.einsum("shqk,skhd->sqhd", dscore, key_f).astype(BF)
    key_grad = jnp.einsum("shqk,sqhd->skhd", dscore, query_f).astype(BF)
    return (
        query_grad.reshape(seq_count, length, width),
        key_grad.reshape(seq_count, length, width),
        value_grad.reshape(seq_count, length, width),
    )


def _pairs(move):
    out = []
    for z in range(NZ):
        for x in range(NX):
            for c in range(NC):
                for s in range(NS):
                    z2, x2, c2, s2 = move(z, x, c, s)
                    source = ((z * NX + x) * NC + c) * NS + s
                    target = (((z2 % NZ) * NX + x2 % NX) * NC + c2) * NS + s2 % NS
                    out.append((source, target))
    return out


def along(first, shift):
    def move(z, x, c, s):
        if (c == 0) == first:
            return z, x + shift, c, s
        return z + shift, x, c, s

    return _pairs(move)


def send(block, pairs):
    return lax.ppermute(block, AXES, pairs)


def send_stage(block, first, shift):
    return send(block, along(first, shift))


def swap_core(block):
    return send(block, _pairs(lambda z, x, c, s: (z, x, 1 - c, s)))


def send_sect(block, shift):
    return send(block, _pairs(lambda z, x, c, s: (z, x, c, s + shift)))


def gather_rows(block):
    near = [block] + [send_stage(block, True, k) for k in (1, 2, 3)]
    near = jnp.concatenate(near, axis=0)
    own = [near] + [send_stage(near, False, k) for k in (1, 2, 3)]
    other = [swap_core(piece) for piece in own]
    return own + other


def _params():
    return pltpu.CompilerParams(vmem_limit_bytes=VMEM)


def _nt(left, right):
    return lax.dot_general(left, right, (((1,), (1,)), ((), ())), preferred_element_type=F32)


def _back_kernel(*refs):
    pieces, w_ref, out_ref = refs[:8], refs[8], refs[9]
    rows = jnp.concatenate([p[...] for p in pieces], axis=0)
    part = _nt(w_ref[...], rows)

    @pl.when(pl.program_id(0) == 0)
    def _():
        out_ref[...] = part

    @pl.when(pl.program_id(0) > 0)
    def _():
        out_ref[...] += part


def back_product(pieces, weight, tile=1024):
    hidden, width = weight.shape[1:]
    rows = sum(p.shape[0] for p in pieces)
    return pl.pallas_call(
        _back_kernel,
        grid=(width // tile,),
        in_specs=[pl.BlockSpec((p.shape[0], tile), lambda i: (0, i)) for p in pieces]
        + [pl.BlockSpec((None, hidden, tile), lambda i: (0, 0, i))],
        out_specs=pl.BlockSpec((hidden, rows), lambda i: (0, 0)),
        out_shape=jax.ShapeDtypeStruct((hidden, rows), F32),
        compiler_params=_params(),
        cost_estimate=pl.CostEstimate(
            flops=2 * hidden * rows * width, bytes_accessed=2 * width * (hidden + rows), transcendentals=0
        ),
    )(*pieces, weight)


def _pre_kernel(*refs):
    pieces, w_ref, back_ref = refs[:8], refs[8], refs[9]
    act_t_ref, grad_t_ref, act_ref, grad_ref, acc_ref = refs[10:]
    rows = jnp.concatenate([p[...] for p in pieces], axis=0)
    part = _nt(w_ref[...], rows)

    @pl.when(pl.program_id(0) == 0)
    def _():
        acc_ref[...] = part

    @pl.when(pl.program_id(0) > 0)
    def _():
        acc_ref[...] += part

    @pl.when(pl.program_id(0) == pl.num_programs(0) - 1)
    def _():
        pre = acc_ref[...]
        sigma = jax.nn.sigmoid(pre)
        act = pre * sigma
        grad = back_ref[...] * sigma * (1.0 + pre * (1.0 - sigma))
        act_t_ref[...] = act.astype(BF)
        grad_t_ref[...] = grad.astype(BF)
        act_ref[...] = act.T.astype(BF)
        grad_ref[...] = grad.T.astype(BF)


def pre_product(pieces, weight, back, tile=1024):
    hidden, width = weight.shape[1:]
    rows = sum(p.shape[0] for p in pieces)
    whole = lambda i: (0, 0)
    return pl.pallas_call(
        _pre_kernel,
        grid=(width // tile,),
        in_specs=[pl.BlockSpec((p.shape[0], tile), lambda i: (0, i)) for p in pieces]
        + [pl.BlockSpec((None, hidden, tile), lambda i: (0, 0, i)), pl.BlockSpec((hidden, rows), whole)],
        out_specs=[pl.BlockSpec((hidden, rows), whole)] * 2 + [pl.BlockSpec((rows, hidden), whole)] * 2,
        out_shape=[jax.ShapeDtypeStruct((hidden, rows), BF)] * 2 + [jax.ShapeDtypeStruct((rows, hidden), BF)] * 2,
        scratch_shapes=[pltpu.VMEM((hidden, rows), F32)],
        compiler_params=_params(),
        cost_estimate=pl.CostEstimate(
            flops=2 * hidden * rows * width, bytes_accessed=2 * width * (hidden + rows), transcendentals=hidden * rows
        ),
    )(*pieces, weight, back)


def _other_kernel(left_ref, w_ref, out_ref):
    out_ref[...] = jnp.dot(left_ref[...], w_ref[...], preferred_element_type=F32).astype(BF)


def other_product(left, weight, tile=1024):
    hidden, width = weight.shape[1:]
    half = left.shape[0] // 2
    return pl.pallas_call(
        _other_kernel,
        grid=(width // tile,),
        in_specs=[
            pl.BlockSpec((half, hidden), lambda i: (1, 0)),
            pl.BlockSpec((None, hidden, tile), lambda i: (0, 0, i)),
        ],
        out_specs=pl.BlockSpec((half, tile), lambda i: (0, i)),
        out_shape=jax.ShapeDtypeStruct((half, width), BF),
        compiler_params=_params(),
        cost_estimate=pl.CostEstimate(
            flops=2 * hidden * half * width, bytes_accessed=2 * width * (hidden + half), transcendentals=0
        ),
    )(left, weight)


def _own_kernel(left_ref, w_ref, in_ref, *out_refs):
    total = jnp.dot(left_ref[...], w_ref[...], preferred_element_type=F32)
    total = total + in_ref[...].astype(F32)
    part = total.shape[0] // 4
    for k, out_ref in enumerate(out_refs):
        out_ref[...] = total[k * part : (k + 1) * part].astype(out_ref.dtype)


def own_product(left, weight, arrived, tile=1024):
    hidden, width = weight.shape[1:]
    half = left.shape[0] // 2
    part = half // 4
    return pl.pallas_call(
        _own_kernel,
        grid=(width // tile,),
        in_specs=[
            pl.BlockSpec((half, hidden), lambda i: (0, 0)),
            pl.BlockSpec((None, hidden, tile), lambda i: (0, 0, i)),
            pl.BlockSpec((half, tile), lambda i: (0, i)),
        ],
        out_specs=[pl.BlockSpec((part, tile), lambda i: (0, i))] * 4,
        out_shape=[jax.ShapeDtypeStruct((part, width), F32)] + [jax.ShapeDtypeStruct((part, width), BF)] * 3,
        compiler_params=_params(),
        cost_estimate=pl.CostEstimate(
            flops=2 * hidden * half * width, bytes_accessed=2 * width * (hidden + 2 * half), transcendentals=0
        ),
    )(left, weight, arrived)


def _grads_kernel(*refs):
    cots, rows = refs[:8], refs[8:16]
    act_ref, grad_ref, up_ref, down_out, up_out, gain_out = refs[16:]
    cot = jnp.concatenate([p[...] for p in cots], axis=0)
    down_out[...] = jnp.dot(act_ref[...], cot, preferred_element_type=F32).astype(BF)
    row = jnp.concatenate([p[...] for p in rows], axis=0)
    up_grad = jnp.dot(grad_ref[...], row, preferred_element_type=F32)
    up_out[...] = up_grad.astype(BF)
    gain_out[...] = jnp.sum(up_grad * up_ref[...].astype(F32), axis=0, keepdims=True)


def grad_products(cots, rows, act_t, grad_t, weight, tile=1024):
    hidden, width = weight.shape[1:]
    count = act_t.shape[1]
    whole = lambda i: (0, 0)
    piece_specs = [pl.BlockSpec((p.shape[0], tile), lambda i: (0, i)) for p in cots]
    weight_spec = pl.BlockSpec((None, hidden, tile), lambda i: (0, 0, i))
    return pl.pallas_call(
        _grads_kernel,
        grid=(width // tile,),
        in_specs=piece_specs * 2 + [pl.BlockSpec((hidden, count), whole)] * 2 + [weight_spec],
        out_specs=[weight_spec, weight_spec, pl.BlockSpec((1, tile), lambda i: (0, i))],
        out_shape=[jax.ShapeDtypeStruct(weight.shape, BF)] * 2 + [jax.ShapeDtypeStruct((1, width), F32)],
        compiler_params=_params(),
        cost_estimate=pl.CostEstimate(
            flops=4 * hidden * count * width,
            bytes_accessed=2 * width * (3 * hidden + 2 * count),
            transcendentals=0,
        ),
    )(*cots, *rows, act_t, grad_t, weight)


def scatter_rows(left, weight):
    arrived = swap_core(other_product(left, weight))
    pieces = own_product(left, weight, arrived)
    total = pieces[0]
    for k in (1, 2, 3):
        total = total + send_stage(pieces[k], False, -k).astype(F32)
    blocks = [total[k * CAP : (k + 1) * CAP] for k in range(4)]
    result = blocks[0]
    for k in (1, 2, 3):
        result = result + send_stage(blocks[k].astype(BF), True, -k).astype(F32)
    return result


def sum_over_dp(row):
    moves = (
        lambda z, x, c, s: (z, x, 1 - c, s),
        lambda z, x, c, s: (z, x ^ 1, c, s),
        lambda z, x, c, s: (z, x ^ 2, c, s),
        lambda z, x, c, s: (z ^ 1, x, c, s),
        lambda z, x, c, s: (z ^ 2, x, c, s),
    )
    for move in moves:
        row = row + send(row, _pairs(move))
    return row


def roll_pieces(pieces, index, axis):
    ordered = [pieces[0], pieces[3], pieces[2], pieces[1]]
    size = pieces[0].shape[axis]
    twice = jnp.concatenate(ordered + ordered[:3], axis=axis)
    start = lax.rem(NS - index, NS) * size
    return lax.dynamic_slice_in_dim(twice, start, NS * size, axis)


def on_device(
    queries, keys, values, residual, labels, slot_modality, gains, up_weight, down_weight, cotangent
):
    slot_index = lax.axis_index("sect")
    token_labels = labels[0]
    length = token_labels.shape[0]
    modality = jnp.sum(jnp.where(jnp.arange(NS) == slot_index, slot_modality, 0))
    keep_mask = token_labels == modality
    before = jnp.arange(length)[:, None] >= jnp.arange(length)[None, :]
    rank_of = jnp.sum(jnp.where(before, keep_mask[None, :], False).astype(jnp.int32), axis=1) - 1
    selector = ((rank_of[None, :] == jnp.arange(CAP)[:, None]) & keep_mask[None, :]).astype(BF)

    def pack(rows):
        return jnp.dot(selector, rows, preferred_element_type=F32).astype(BF)

    grad_full = cotangent[0]
    cot_rows = gather_rows(pack(grad_full))

    attended_block, probs, probs_b = causal_forward(queries, keys, values)
    block = attended_block[0]
    attended = roll_pieces([block] + [send_sect(block, k) for k in (1, 2, 3)], slot_index, 1)
    hidden = (residual[0].astype(F32) + attended.astype(F32)).astype(BF)
    hidden_f = hidden.astype(F32)
    onehot = (token_labels[:, None] == jnp.arange(MODALITIES)[None, :]).astype(F32)
    gain_rows = jnp.dot(onehot, gains, precision=lax.Precision.HIGHEST)
    inverse = lax.rsqrt(jnp.mean(hidden_f * hidden_f, axis=-1, keepdims=True) + 1e-05)
    normed = (hidden_f * inverse * gain_rows).astype(BF)
    token_rows = gather_rows(pack(normed))

    back = back_product(cot_rows, down_weight)
    act_t, grad_t, act, grad = pre_product(token_rows, up_weight, back)
    ffn_rows = scatter_rows(act, down_weight)
    norm_rows = scatter_rows(grad, up_weight)
    down_grad, up_grad, gain_part = grad_products(cot_rows, token_rows, act_t, grad_t, up_weight)

    gain_sum = sum_over_dp(gain_part)
    gain_grad = jnp.zeros(gains.shape, F32)
    for k in range(NS):
        part = gain_sum if k == 0 else send_sect(gain_sum, k)
        owner = lax.rem(slot_index - k + NS, NS)
        kind = jnp.sum(jnp.where(jnp.arange(NS) == owner, slot_modality, 0))
        gain_grad = gain_grad + jnp.where(jnp.arange(MODALITIES)[:, None] == kind, part, 0.0)
    gain_grad = gain_grad / gains

    quarter = length // NS
    rows_two = jnp.concatenate([ffn_rows, norm_rows], axis=1).astype(BF)
    spread = jnp.dot(selector.T, rows_two, preferred_element_type=F32).astype(BF)

    def own_quarter(array, shift=0):
        return lax.dynamic_slice_in_dim(array, lax.rem(slot_index + shift, NS) * quarter, quarter, 0)

    total = own_quarter(spread).astype(F32)
    for k in (1, 2, 3):
        total = total + send_sect(own_quarter(spread, k), k).astype(F32)
    width = hidden.shape[1]
    ffn, norm_grad = total[:, :width], total[:, width:]
    hidden_q = own_quarter(hidden).astype(F32)
    output = (hidden_q + ffn).astype(BF)[None]
    normed_q = hidden_q * own_quarter(inverse)
    scaled = norm_grad * own_quarter(gain_rows)
    hidden_grad = own_quarter(grad_full).astype(F32) + own_quarter(inverse) * (
        scaled - normed_q * jnp.mean(scaled * normed_q, axis=-1, keepdims=True)
    )
    residual_grad = hidden_grad.astype(BF)
    block_width = queries.shape[2]

    def columns(shift):
        start = lax.rem(slot_index + shift, NS) * block_width
        return lax.dynamic_slice_in_dim(residual_grad, start, block_width, 1)

    grad_block = roll_pieces([columns(0)] + [send_sect(columns(k), k) for k in (1, 2, 3)], slot_index, 0)[None]
    query_grad, key_grad, value_grad = causal_backward(
        grad_block, queries, keys, values, attended_block, probs, probs_b
    )
    return (
        output,
        residual_grad[None],
        query_grad,
        key_grad,
        value_grad,
        up_grad,
        down_grad,
        gain_grad,
    )


def solution(mesh):
    in_specs = (
        P("dp", None, "sect"),
        P("dp", None, "sect"),
        P("dp", None, "sect"),
        P("dp", None, None),
        P("dp", None),
        P(),
        P(),
        P("sect", "dp", None),
        P("sect", "dp", None),
        P("dp", None, None),
    )
    out_specs = (
        P("dp", "sect", None),
        P("dp", "sect", None),
        P("dp", None, "sect"),
        P("dp", None, "sect"),
        P("dp", None, "sect"),
        P("sect", "dp", None),
        P("sect", "dp", None),
        P(),
    )
    return jax.shard_map(
        on_device, mesh=mesh, in_specs=in_specs, out_specs=out_specs, check_vma=False
    )
```

```python
import functools

import jax
import jax.numpy as jnp
from jax import lax
from jax.experimental import pallas as pl
from jax.experimental.pallas import tpu as pltpu
from jax.sharding import PartitionSpec as P

HD = 128
MODALITIES = 3
NZ = 4
NX = 4
NC = 2
NS = 4
AXES = ("dp", "sect")
BF = jnp.bfloat16
F32 = jnp.float32
CAP = 8
VMEM = 60 * 1024 * 1024


def causal_forward(queries, keys, values):
    seq_count, length, width = queries.shape
    head_count = width // HD
    query_f = queries.astype(F32).reshape(seq_count, length, head_count, HD)
    key_f = keys.astype(F32).reshape(seq_count, length, head_count, HD)
    value_f = values.astype(F32).reshape(seq_count, length, head_count, HD)
    scores = jnp.einsum("sqhd,skhd->shqk", query_f, key_f) * HD ** (-0.5)
    position = jnp.arange(length)
    causal = position[:, None] >= position[None, :]
    scores = jnp.where(causal, scores, -1e30)
    probs = jax.nn.softmax(scores, axis=-1)
    probs_b = probs.astype(BF)
    attended = jnp.einsum("shqk,skhd->sqhd", probs_b.astype(F32), value_f)
    return (attended.astype(BF).reshape(seq_count, length, width), probs, probs_b)


def causal_backward(grad_out, queries, keys, values, attended, probs, probs_b):
    seq_count, length, width = queries.shape
    head_count = width // HD
    shape = (seq_count, length, head_count, HD)
    grad_f = grad_out.astype(F32).reshape(shape)
    query_f = queries.astype(F32).reshape(shape)
    key_f = keys.astype(F32).reshape(shape)
    value_f = values.astype(F32).reshape(shape)
    attended_f = attended.astype(F32).reshape(shape)
    value_grad = jnp.einsum("shqk,sqhd->skhd", probs_b.astype(F32), grad_f).astype(BF)
    dprob = jnp.einsum("sqhd,skhd->shqk", grad_f, value_f)
    delta = jnp.einsum("sqhd,sqhd->shq", grad_f, attended_f)
    dscore = (probs * (dprob - delta[..., None]) * HD ** (-0.5)).astype(BF).astype(F32)
    query_grad = jnp.einsum("shqk,skhd->sqhd", dscore, key_f).astype(BF)
    key_grad = jnp.einsum("shqk,sqhd->skhd", dscore, query_f).astype(BF)
    return (
        query_grad.reshape(seq_count, length, width),
        key_grad.reshape(seq_count, length, width),
        value_grad.reshape(seq_count, length, width),
    )


def _pairs(move):
    out = []
    for z in range(NZ):
        for x in range(NX):
            for c in range(NC):
                for s in range(NS):
                    z2, x2, c2, s2 = move(z, x, c, s)
                    source = ((z * NX + x) * NC + c) * NS + s
                    target = (((z2 % NZ) * NX + x2 % NX) * NC + c2) * NS + s2 % NS
                    out.append((source, target))
    return out


def along(first, shift):
    def move(z, x, c, s):
        if (c == 0) == first:
            return z, x + shift, c, s
        return z + shift, x, c, s

    return _pairs(move)


def send(block, pairs):
    return lax.ppermute(block, AXES, pairs)


def send_stage(block, first, shift):
    return send(block, along(first, shift))


def swap_core(block):
    return send(block, _pairs(lambda z, x, c, s: (z, x, 1 - c, s)))


def send_sect(block, shift):
    return send(block, _pairs(lambda z, x, c, s: (z, x, c, s + shift)))


def gather_rows(block):
    near = [block] + [send_stage(block, True, k) for k in (1, 2, 3)]
    near = jnp.concatenate(near, axis=0)
    own = [near] + [send_stage(near, False, k) for k in (1, 2, 3)]
    other = [swap_core(piece) for piece in own]
    return own + other


def _params(limit=VMEM):
    return pltpu.CompilerParams(vmem_limit_bytes=limit)


def _nt(left, right):
    return lax.dot_general(left, right, (((1,), (1,)), ((), ())), preferred_element_type=F32)


def _slot_selector(labels, kind):
    length = labels.shape[1]
    keep = jnp.broadcast_to((labels == kind).astype(F32), (CAP, length))
    first = lax.broadcasted_iota(jnp.int32, (length, length), 0)
    second = lax.broadcasted_iota(jnp.int32, (length, length), 1)
    rank = jnp.dot(keep, (first <= second).astype(F32), preferred_element_type=F32)
    row = lax.broadcasted_iota(jnp.int32, (CAP, length), 0).astype(F32)
    return jnp.where((rank == row + 1.0) & (keep > 0.5), 1.0, 0.0)


def _slot_spreader(labels, kind):
    length = labels.shape[0]
    keep = jnp.broadcast_to((labels == kind).astype(F32), (length, CAP))
    first = lax.broadcasted_iota(jnp.int32, (length, length), 0)
    second = lax.broadcasted_iota(jnp.int32, (length, length), 1)
    rank = jnp.dot((second <= first).astype(F32), keep, preferred_element_type=F32)
    column = lax.broadcasted_iota(jnp.int32, (length, CAP), 1).astype(F32)
    return jnp.where((rank == column + 1.0) & (keep > 0.5), 1.0, 0.0)


SMALL_COST = pl.CostEstimate(flops=1000, bytes_accessed=1000, transcendentals=0)
SMALL = pl.BlockSpec(memory_space=pltpu.SMEM)
def _whole(*arrays):
    return [pl.BlockSpec(a.shape, lambda i, n=len(a.shape): (0,) * n) for a in arrays]


RAW = pl.BlockSpec(memory_space=pl.ANY)


def _pack_kernel(slot_ref, kinds_ref, labels_ref, rows_ref, out_ref):
    select = _slot_selector(labels_ref[...], kinds_ref[slot_ref[0]]).astype(BF)
    out_ref[...] = jnp.dot(select, rows_ref[...], preferred_element_type=F32).astype(BF)


def pack_rows(slot, kinds, labels, rows):
    out = jax.ShapeDtypeStruct((CAP, rows.shape[1]), BF)
    return pl.pallas_call(
        _pack_kernel,
        grid=(1,),
        in_specs=[SMALL, SMALL] + _whole(labels, rows),
        out_specs=_whole(out)[0],
        out_shape=out,
        compiler_params=_params(8 * 1024 * 1024),
        cost_estimate=SMALL_COST,
    )(slot, kinds, labels, rows)


def _gain_rows(labels, gains):
    return jnp.where(labels == 0, gains[0:1], jnp.where(labels == 1, gains[1:2], gains[2:3]))


def _norm_kernel(slot_ref, kinds_ref, labels_ref, column_ref, residual_ref, gains_ref, *refs):
    blocks, (hidden_ref, packed_ref, joined_ref) = refs[:NS], refs[NS:]
    slot = slot_ref[0]
    width = blocks[0].shape[1]
    for k, block in enumerate(blocks):
        owner = lax.rem(slot - k + NS, NS)
        joined_ref[:, pl.ds(pl.multiple_of(owner * width, width), width)] = block[...]
    hidden = (residual_ref[...].astype(F32) + joined_ref[...].astype(F32)).astype(BF)
    hidden_ref[...] = hidden
    hidden_f = hidden.astype(F32)
    inverse = lax.rsqrt(jnp.mean(hidden_f * hidden_f, axis=-1, keepdims=True) + 1e-05)
    normed = (hidden_f * inverse * _gain_rows(column_ref[...], gains_ref[...])).astype(BF)
    select = _slot_selector(labels_ref[...], kinds_ref[slot]).astype(BF)
    packed_ref[...] = jnp.dot(select, normed, preferred_element_type=F32).astype(BF)


def norm_rows_of(slot, kinds, labels, column, residual, gains, blocks):
    length, width = residual.shape
    outs = [jax.ShapeDtypeStruct((length, width), BF), jax.ShapeDtypeStruct((CAP, width), BF)]
    return pl.pallas_call(
        _norm_kernel,
        grid=(1,),
        in_specs=[SMALL, SMALL] + _whole(labels, column, residual, gains, *blocks),
        out_specs=_whole(*outs),
        out_shape=outs,
        scratch_shapes=[pltpu.VMEM((length, width), BF)],
        compiler_params=_params(8 * 1024 * 1024),
        cost_estimate=SMALL_COST,
    )(slot, kinds, labels, column, residual, gains, *blocks)


def _finish_kernel(slot_ref, kinds_ref, column_ref, hidden_ref, cot_ref, gains_ref, *refs):
    sums, (quarter_ref, block_ref, full_ref) = refs[:NS], refs[NS:]
    slot = slot_ref[0]
    labels = column_ref[...]
    spreaders = [
        _slot_spreader(labels, kinds_ref[lax.rem(slot - k + NS, NS)]) for k in range(NS)
    ]
    spread = jnp.concatenate(spreaders, axis=1).astype(BF)
    rows = jnp.concatenate([s[...].astype(F32) for s in sums], axis=0).astype(BF)
    norm_grad = jnp.dot(spread, rows, preferred_element_type=F32)
    hidden_f = hidden_ref[...].astype(F32)
    inverse = lax.rsqrt(jnp.mean(hidden_f * hidden_f, axis=-1, keepdims=True) + 1e-05)
    normed_f = hidden_f * inverse
    scaled = norm_grad * _gain_rows(labels, gains_ref[...])
    centre = jnp.mean(scaled * normed_f, axis=-1, keepdims=True)
    full = (cot_ref[...].astype(F32) + inverse * (scaled - normed_f * centre)).astype(BF)
    full_ref[...] = full
    width = block_ref.shape[1]
    block_ref[...] = full_ref[:, pl.ds(pl.multiple_of(slot * width, width), width)]
    wide = full.astype(F32)
    count = quarter_ref.shape[0]
    quarter = wide[:count]
    for t in range(1, NS):
        quarter = jnp.where(slot == t, wide[t * count : (t + 1) * count], quarter)
    quarter_ref[...] = quarter.astype(BF)


def finish_norm(slot, kinds, column, hidden, cot, gains, sums, block_width):
    length, width = hidden.shape
    outs = [
        jax.ShapeDtypeStruct((length // NS, width), BF),
        jax.ShapeDtypeStruct((length, block_width), BF),
    ]
    return pl.pallas_call(
        _finish_kernel,
        grid=(1,),
        in_specs=[SMALL, SMALL] + _whole(column, hidden, cot, gains, *sums),
        out_specs=_whole(*outs),
        out_shape=outs,
        scratch_shapes=[pltpu.VMEM((length, width), BF)],
        compiler_params=_params(12 * 1024 * 1024),
        cost_estimate=SMALL_COST,
    )(slot, kinds, column, hidden, cot, gains, *sums)


def _back_kernel(*refs):
    pieces, w_ref, out_ref = refs[:8], refs[8], refs[9]
    rows = jnp.concatenate([p[...] for p in pieces], axis=0)
    part = _nt(w_ref[...], rows)

    @pl.when(pl.program_id(0) == 0)
    def _():
        out_ref[...] = part

    @pl.when(pl.program_id(0) > 0)
    def _():
        out_ref[...] += part


def back_product(pieces, weight, tile=4096):
    hidden, width = weight.shape[1:]
    rows = sum(p.shape[0] for p in pieces)
    return pl.pallas_call(
        _back_kernel,
        grid=(width // tile,),
        in_specs=[pl.BlockSpec((p.shape[0], tile), lambda i: (0, i)) for p in pieces]
        + [pl.BlockSpec((None, hidden, tile), lambda i: (0, 0, i))],
        out_specs=pl.BlockSpec((hidden, rows), lambda i: (0, 0)),
        out_shape=jax.ShapeDtypeStruct((hidden, rows), F32),
        compiler_params=_params(),
        cost_estimate=SMALL_COST,
    )(*pieces, weight)


CHUNKS = 2
STEP = 1024
OUT_STEP = 2048


def _pre_kernel(*refs):
    pieces, w_hbm, back_ref = refs[:8], refs[8], refs[9]
    act_t_ref, grad_t_ref, act_ref, grad_ref, other_hbm = refs[10:15]
    rows_ref, w_ref, acc_ref, other_ref, sems, out_sems = refs[15:]
    width = w_ref.shape[1]
    size = width // CHUNKS
    part = pieces[0].shape[0]
    copies = []
    for c in range(CHUNKS):
        span = pl.ds(c * size, size)
        group = [pltpu.make_async_copy(w_hbm.at[0, :, span], w_ref.at[:, span], sems.at[c, 8])]
        for p, piece in enumerate(pieces):
            group.append(
                pltpu.make_async_copy(
                    piece.at[:, span], rows_ref.at[pl.ds(p * part, part), span], sems.at[c, p]
                )
            )
        for copy in group:
            copy.start()
        copies.append(group)
    acc_ref[...] = jnp.zeros_like(acc_ref)
    for c in range(CHUNKS):
        for copy in copies[c]:
            copy.wait()

        @pl.loop(0, size // STEP)
        def _(i):
            span = pl.ds(pl.multiple_of(c * size + i * STEP, STEP), STEP)
            acc_ref[...] += _nt(w_ref[:, span], rows_ref[:, span])

    pre = acc_ref[...]
    sigma = jax.nn.sigmoid(pre)
    act = pre * sigma
    grad = back_ref[...] * sigma * (1.0 + pre * (1.0 - sigma))
    grad_t_ref[...] = grad.astype(BF)
    grad_ref[...] = grad.T.astype(BF)
    half = other_ref.shape[0]
    left = grad_ref[half:, :]
    outs = []
    for n in range(width // OUT_STEP):
        span = pl.ds(n * OUT_STEP, OUT_STEP)
        other_ref[:, span] = jnp.dot(left, w_ref[:, span], preferred_element_type=F32).astype(BF)
        copy = pltpu.make_async_copy(other_ref.at[:, span], other_hbm.at[:, span], out_sems.at[n])
        copy.start()
        outs.append(copy)
    act_t_ref[...] = act.astype(BF)
    act_ref[...] = act.T.astype(BF)
    for copy in outs:
        copy.wait()


def pre_product(pieces, weight, back):
    hidden, width = weight.shape[1:]
    rows = sum(p.shape[0] for p in pieces)
    outs = (
        [jax.ShapeDtypeStruct((hidden, rows), BF)] * 2
        + [jax.ShapeDtypeStruct((rows, hidden), BF)] * 2
        + [jax.ShapeDtypeStruct((rows // 2, width), BF)]
    )
    return pl.pallas_call(
        _pre_kernel,
        grid=(1,),
        in_specs=[RAW] * 9 + _whole(back),
        out_specs=_whole(*outs[:4]) + [RAW],
        out_shape=outs,
        scratch_shapes=[
            pltpu.VMEM((rows, width), BF),
            pltpu.VMEM((hidden, width), BF),
            pltpu.VMEM((hidden, rows), F32),
            pltpu.VMEM((rows // 2, width), BF),
            pltpu.SemaphoreType.DMA((CHUNKS, 9)),
            pltpu.SemaphoreType.DMA((width // OUT_STEP,)),
        ],
        compiler_params=_params(),
        cost_estimate=SMALL_COST,
    )(*pieces, weight, back)


def _other_kernel(left_ref, w_ref, out_ref):
    out_ref[...] = jnp.dot(left_ref[...], w_ref[...], preferred_element_type=F32).astype(BF)


def other_product(left, weight, tile=4096):
    hidden, width = weight.shape[1:]
    half = left.shape[0] // 2
    return pl.pallas_call(
        _other_kernel,
        grid=(width // tile,),
        in_specs=[
            pl.BlockSpec((half, hidden), lambda i: (1, 0)),
            pl.BlockSpec((None, hidden, tile), lambda i: (0, 0, i)),
        ],
        out_specs=pl.BlockSpec((half, tile), lambda i: (0, i)),
        out_shape=jax.ShapeDtypeStruct((half, width), BF),
        compiler_params=_params(),
        cost_estimate=SMALL_COST,
    )(left, weight)


def _own_kernel(*refs):
    left_ref, w_ref, in_ref = refs[:3]
    rows, outs = refs[3:-4], refs[-4:]
    total = jnp.dot(left_ref[...], w_ref[...], preferred_element_type=F32)
    total = total + in_ref[...].astype(F32)
    part = total.shape[0] // 4
    if rows:
        rows, gain_ref, outs = rows[:4], rows[4], outs
        gain = None
        for k, row_ref in enumerate(rows):
            term = jnp.sum(row_ref[...].astype(F32) * total[k * part : (k + 1) * part], axis=0, keepdims=True)
            gain = term if gain is None else gain + term
        gain_ref[...] = gain
    for k, out_ref in enumerate(outs):
        out_ref[...] = total[k * part : (k + 1) * part].astype(out_ref.dtype)


def own_product(left, weight, arrived, rows=(), tile=4096):
    hidden, width = weight.shape[1:]
    half = left.shape[0] // 2
    part = half // 4
    piece = pl.BlockSpec((part, tile), lambda i: (0, i))
    gain_spec = [pl.BlockSpec((1, tile), lambda i: (0, i))] if rows else []
    gain_shape = [jax.ShapeDtypeStruct((1, width), F32)] if rows else []
    return pl.pallas_call(
        _own_kernel,
        grid=(width // tile,),
        in_specs=[
            pl.BlockSpec((half, hidden), lambda i: (0, 0)),
            pl.BlockSpec((None, hidden, tile), lambda i: (0, 0, i)),
            pl.BlockSpec((half, tile), lambda i: (0, i)),
        ]
        + [piece] * len(rows),
        out_specs=gain_spec + [piece] * 4,
        out_shape=gain_shape
        + [jax.ShapeDtypeStruct((part, width), F32)]
        + [jax.ShapeDtypeStruct((part, width), BF)] * 3,
        compiler_params=_params(),
        cost_estimate=SMALL_COST,
    )(left, weight, arrived, *rows)


def _grads_kernel(*refs):
    cots, rows = refs[:8], refs[8:16]
    act_ref, grad_ref, down_out, up_out = refs[16:]
    cot = jnp.concatenate([p[...] for p in cots], axis=0)
    down_out[...] = jnp.dot(act_ref[...], cot, preferred_element_type=F32).astype(BF)
    row = jnp.concatenate([p[...] for p in rows], axis=0)
    up_out[...] = jnp.dot(grad_ref[...], row, preferred_element_type=F32).astype(BF)


def grad_products(cots, rows, act_t, grad_t, shape, tile=2048):
    _, hidden, width = shape
    count = act_t.shape[1]
    whole = lambda i: (0, 0)
    piece_specs = [pl.BlockSpec((p.shape[0], tile), lambda i: (0, i)) for p in cots]
    weight_spec = pl.BlockSpec((None, hidden, tile), lambda i: (0, 0, i))
    return pl.pallas_call(
        _grads_kernel,
        grid=(width // tile,),
        in_specs=piece_specs * 2 + [pl.BlockSpec((hidden, count), whole)] * 2,
        out_specs=[weight_spec, weight_spec],
        out_shape=[jax.ShapeDtypeStruct(shape, BF)] * 2,
        compiler_params=_params(),
        cost_estimate=pl.CostEstimate(
            flops=4 * hidden * count * width,
            bytes_accessed=2 * width * (2 * hidden + 2 * count),
            transcendentals=0,
        ),
    )(*cots, *rows, act_t, grad_t)


def far_sum(pieces):
    total = pieces[0]
    for k in (1, 2, 3):
        total = total + send_stage(pieces[k], False, -k).astype(F32)
    return total


def near_sum(total, dtype):
    blocks = [total[k * CAP : (k + 1) * CAP] for k in range(4)]
    result = blocks[0]
    for k in (1, 2, 3):
        result = result + send_stage(blocks[k].astype(dtype), True, -k).astype(F32)
    return result


def sum_over_dp(row):
    moves = (
        lambda z, x, c, s: (z, x, 1 - c, s),
        lambda z, x, c, s: (z, x ^ 1, c, s),
        lambda z, x, c, s: (z, x ^ 2, c, s),
        lambda z, x, c, s: (z ^ 1, x, c, s),
        lambda z, x, c, s: (z ^ 2, x, c, s),
    )
    for move in moves:
        row = row + send(row, _pairs(move))
    return row


def after(value, *others):
    return lax.optimization_barrier((value, *others))[0]


def on_device(
    queries, keys, values, residual, labels, slot_modality, gains, up_weight, down_weight, cotangent
):
    slot_index = lax.axis_index("sect")
    slot = slot_index.astype(jnp.int32).reshape(1)
    column = labels.reshape(-1, 1)
    length = labels.shape[1]
    grad_full = cotangent[0]
    packed_cot = pack_rows(slot, slot_modality, labels, grad_full)
    cot_rows = gather_rows(packed_cot)
    queries, keys, values, _ = lax.optimization_barrier((queries, keys, values, packed_cot))

    attended_block, probs, probs_b = causal_forward(queries, keys, values)
    block = attended_block[0]
    blocks = [block] + [send_sect(block, k) for k in (1, 2, 3)]
    hidden, packed = norm_rows_of(slot, slot_modality, labels, column, residual[0], gains, blocks)
    token_rows = gather_rows(packed)

    back = back_product(cot_rows, down_weight)
    act_t, grad_t, act, grad, norm_other = pre_product(token_rows, up_weight, back)
    norm_arrived = swap_core(norm_other)
    ffn_other = other_product(after(act, norm_other), down_weight)
    ffn_arrived = swap_core(ffn_other)
    gain_part, *norm_pieces = own_product(after(grad, ffn_other), up_weight, norm_arrived, token_rows[:4])
    ffn_pieces = own_product(after(act, norm_pieces[0]), down_weight, ffn_arrived)
    down_grad, up_grad = grad_products(
        cot_rows, token_rows, after(act_t, ffn_pieces[0]), grad_t, up_weight.shape
    )
    norm_total = far_sum(norm_pieces)
    norm_rows = near_sum(norm_total, F32).astype(BF)
    sums = [norm_rows] + [send_sect(norm_rows, k) for k in (1, 2, 3)]
    residual_grad, grad_block = finish_norm(
        slot, slot_modality, column, hidden, grad_full, gains, sums, queries.shape[2]
    )
    query_grad, key_grad, value_grad = causal_backward(
        grad_block[None], queries, keys, values, attended_block, probs, probs_b
    )

    gain_sum = sum_over_dp(after(gain_part, norm_total))
    gain_grad = jnp.zeros(gains.shape, F32)
    for k in range(NS):
        part = gain_sum if k == 0 else send_sect(gain_sum, k)
        owner = lax.rem(slot_index - k + NS, NS)
        kind = jnp.sum(jnp.where(jnp.arange(NS) == owner, slot_modality, 0))
        gain_grad = gain_grad + jnp.where(jnp.arange(MODALITIES)[:, None] == kind, part, 0.0)
    gain_grad = gain_grad / gains

    quarter = length // NS
    ffn_rows = near_sum(far_sum(ffn_pieces), BF).astype(BF)
    keep = labels[0] == jnp.sum(jnp.where(jnp.arange(NS) == slot_index, slot_modality, 0))
    before = jnp.arange(length)[:, None] >= jnp.arange(length)[None, :]
    rank_of = jnp.sum(jnp.where(before, keep[None, :], False).astype(jnp.int32), axis=1) - 1
    spreader = ((rank_of[:, None] == jnp.arange(CAP)[None, :]) & keep[:, None]).astype(BF)
    spread = jnp.dot(spreader, ffn_rows, preferred_element_type=F32).astype(BF)

    def own_quarter(array, shift=0):
        return lax.dynamic_slice_in_dim(array, lax.rem(slot_index + shift, NS) * quarter, quarter, 0)

    total = own_quarter(spread).astype(F32)
    for k in (1, 2, 3):
        total = total + send_sect(own_quarter(spread, k), k).astype(F32)
    output = (own_quarter(hidden).astype(F32) + total).astype(BF)[None]
    return (
        output,
        residual_grad[None],
        query_grad,
        key_grad,
        value_grad,
        up_grad,
        down_grad,
        gain_grad,
    )


def solution(mesh):
    in_specs = (
        P("dp", None, "sect"),
        P("dp", None, "sect"),
        P("dp", None, "sect"),
        P("dp", None, None),
        P("dp", None),
        P(),
        P(),
        P("sect", "dp", None),
        P("sect", "dp", None),
        P("dp", None, None),
    )
    out_specs = (
        P("dp", "sect", None),
        P("dp", "sect", None),
        P("dp", None, "sect"),
        P("dp", None, "sect"),
        P("dp", None, "sect"),
        P("sect", "dp", None),
        P("sect", "dp", None),
        P(),
    )
    return jax.shard_map(
        on_device, mesh=mesh, in_specs=in_specs, out_specs=out_specs, check_vma=False
    )
```

```python
import functools

import jax
import jax.numpy as jnp
from jax import lax
from jax.experimental import pallas as pl
from jax.experimental.pallas import tpu as pltpu
from jax.sharding import PartitionSpec as P

HD = 128
MODALITIES = 3
NZ = 4
NX = 4
NC = 2
NS = 4
AXES = ("dp", "sect")
BF = jnp.bfloat16
F32 = jnp.float32
CAP = 8
VMEM = 46 * 1024 * 1024


def causal_forward(queries, keys, values):
    seq_count, length, width = queries.shape
    head_count = width // HD
    query_f = queries.astype(F32).reshape(seq_count, length, head_count, HD)
    key_f = keys.astype(F32).reshape(seq_count, length, head_count, HD)
    value_f = values.astype(F32).reshape(seq_count, length, head_count, HD)
    scores = jnp.einsum("sqhd,skhd->shqk", query_f, key_f) * HD ** (-0.5)
    position = jnp.arange(length)
    causal = position[:, None] >= position[None, :]
    scores = jnp.where(causal, scores, -1e30)
    probs = jax.nn.softmax(scores, axis=-1)
    probs_b = probs.astype(BF)
    attended = jnp.einsum("shqk,skhd->sqhd", probs_b.astype(F32), value_f)
    return (attended.astype(BF).reshape(seq_count, length, width), probs, probs_b)


def causal_backward(grad_out, queries, keys, values, attended, probs, probs_b):
    seq_count, length, width = queries.shape
    head_count = width // HD
    shape = (seq_count, length, head_count, HD)
    grad_f = grad_out.astype(F32).reshape(shape)
    query_f = queries.astype(F32).reshape(shape)
    key_f = keys.astype(F32).reshape(shape)
    value_f = values.astype(F32).reshape(shape)
    attended_f = attended.astype(F32).reshape(shape)
    value_grad = jnp.einsum("shqk,sqhd->skhd", probs_b.astype(F32), grad_f).astype(BF)
    dprob = jnp.einsum("sqhd,skhd->shqk", grad_f, value_f)
    delta = jnp.einsum("sqhd,sqhd->shq", grad_f, attended_f)
    dscore = (probs * (dprob - delta[..., None]) * HD ** (-0.5)).astype(BF).astype(F32)
    query_grad = jnp.einsum("shqk,skhd->sqhd", dscore, key_f).astype(BF)
    key_grad = jnp.einsum("shqk,sqhd->skhd", dscore, query_f).astype(BF)
    return (
        query_grad.reshape(seq_count, length, width),
        key_grad.reshape(seq_count, length, width),
        value_grad.reshape(seq_count, length, width),
    )


def _pairs(move):
    out = []
    for z in range(NZ):
        for x in range(NX):
            for c in range(NC):
                for s in range(NS):
                    z2, x2, c2, s2 = move(z, x, c, s)
                    source = ((z * NX + x) * NC + c) * NS + s
                    target = (((z2 % NZ) * NX + x2 % NX) * NC + c2) * NS + s2 % NS
                    out.append((source, target))
    return out


def along(first, shift):
    def move(z, x, c, s):
        if (c == 0) == first:
            return z, x + shift, c, s
        return z + shift, x, c, s

    return _pairs(move)


def send(block, pairs):
    return lax.ppermute(block, AXES, pairs)


def send_stage(block, first, shift):
    return send(block, along(first, shift))


def swap_core(block):
    return send(block, _pairs(lambda z, x, c, s: (z, x, 1 - c, s)))


def send_sect(block, shift):
    return send(block, _pairs(lambda z, x, c, s: (z, x, c, s + shift)))


def gather_near(block):
    return jnp.concatenate([block] + [send_stage(block, True, k) for k in (1, 2, 3)], axis=0)


def gather_far(near):
    return [near] + [send_stage(near, False, k) for k in (1, 2, 3)]


def _params(limit=VMEM):
    return pltpu.CompilerParams(vmem_limit_bytes=limit)


def _nt(left, right):
    return lax.dot_general(left, right, (((1,), (1,)), ((), ())), preferred_element_type=F32)


def _slot_selector(labels, kind):
    length = labels.shape[1]
    keep = jnp.broadcast_to((labels == kind).astype(F32), (CAP, length))
    first = lax.broadcasted_iota(jnp.int32, (length, length), 0)
    second = lax.broadcasted_iota(jnp.int32, (length, length), 1)
    rank = jnp.dot(keep, (first <= second).astype(F32), preferred_element_type=F32)
    row = lax.broadcasted_iota(jnp.int32, (CAP, length), 0).astype(F32)
    return jnp.where((rank == row + 1.0) & (keep > 0.5), 1.0, 0.0)


def _slot_spreader(labels, kind):
    length = labels.shape[0]
    keep = jnp.broadcast_to((labels == kind).astype(F32), (length, CAP))
    first = lax.broadcasted_iota(jnp.int32, (length, length), 0)
    second = lax.broadcasted_iota(jnp.int32, (length, length), 1)
    rank = jnp.dot((second <= first).astype(F32), keep, preferred_element_type=F32)
    column = lax.broadcasted_iota(jnp.int32, (length, CAP), 1).astype(F32)
    return jnp.where((rank == column + 1.0) & (keep > 0.5), 1.0, 0.0)


SMALL_COST = pl.CostEstimate(flops=1000, bytes_accessed=1000, transcendentals=0)
SMALL = pl.BlockSpec(memory_space=pltpu.SMEM)
def _whole(*arrays):
    return [pl.BlockSpec(a.shape, lambda i, n=len(a.shape): (0,) * n) for a in arrays]


RAW = pl.BlockSpec(memory_space=pl.ANY)


def _pack_kernel(slot_ref, kinds_ref, labels_ref, rows_ref, out_ref):
    select = _slot_selector(labels_ref[...], kinds_ref[slot_ref[0]]).astype(BF)
    out_ref[...] = jnp.dot(select, rows_ref[...], preferred_element_type=F32).astype(BF)


def pack_rows(slot, kinds, labels, rows):
    out = jax.ShapeDtypeStruct((CAP, rows.shape[1]), BF)
    return pl.pallas_call(
        _pack_kernel,
        grid=(1,),
        in_specs=[SMALL, SMALL] + _whole(labels, rows),
        out_specs=_whole(out)[0],
        out_shape=out,
        compiler_params=_params(),
        cost_estimate=SMALL_COST,
    )(slot, kinds, labels, rows)


def _gain_rows(labels, gains):
    return jnp.where(labels == 0, gains[0:1], jnp.where(labels == 1, gains[1:2], gains[2:3]))


def _norm_kernel(slot_ref, kinds_ref, labels_ref, column_ref, residual_ref, gains_ref, *refs):
    blocks, (hidden_ref, packed_ref, joined_ref) = refs[:NS], refs[NS:]
    slot = slot_ref[0]
    width = blocks[0].shape[1]
    for k, block in enumerate(blocks):
        owner = lax.rem(slot - k + NS, NS)
        joined_ref[:, pl.ds(pl.multiple_of(owner * width, width), width)] = block[...]
    hidden = (residual_ref[...].astype(F32) + joined_ref[...].astype(F32)).astype(BF)
    hidden_ref[...] = hidden
    hidden_f = hidden.astype(F32)
    inverse = lax.rsqrt(jnp.mean(hidden_f * hidden_f, axis=-1, keepdims=True) + 1e-05)
    normed = (hidden_f * inverse * _gain_rows(column_ref[...], gains_ref[...])).astype(BF)
    select = _slot_selector(labels_ref[...], kinds_ref[slot]).astype(BF)
    packed_ref[...] = jnp.dot(select, normed, preferred_element_type=F32).astype(BF)


def norm_rows_of(slot, kinds, labels, column, residual, gains, blocks):
    length, width = residual.shape
    outs = [jax.ShapeDtypeStruct((length, width), BF), jax.ShapeDtypeStruct((CAP, width), BF)]
    return pl.pallas_call(
        _norm_kernel,
        grid=(1,),
        in_specs=[SMALL, SMALL] + _whole(labels, column, residual, gains, *blocks),
        out_specs=_whole(*outs),
        out_shape=outs,
        scratch_shapes=[pltpu.VMEM((length, width), BF)],
        compiler_params=_params(),
        cost_estimate=SMALL_COST,
    )(slot, kinds, labels, column, residual, gains, *blocks)


def _finish_kernel(slot_ref, kinds_ref, column_ref, hidden_ref, cot_ref, gains_ref, *refs):
    sums, (quarter_ref, block_ref, gain_ref, full_ref) = refs[:NS], refs[NS:]
    slot = slot_ref[0]
    labels = column_ref[...]
    kinds = [kinds_ref[lax.rem(slot - k + NS, NS)] for k in range(NS)]
    spreaders = [_slot_spreader(labels, kind) for kind in kinds]
    spread = jnp.concatenate(spreaders, axis=1).astype(BF)
    wide = hidden_ref.shape[1]
    rows = jnp.concatenate([s[:, :wide].astype(F32) for s in sums], axis=0).astype(BF)
    extra = wide // CAP
    parts = [
        s[:, wide : wide + extra].astype(F32) + s[:, wide + extra :].astype(F32) for s in sums
    ]
    for m in range(MODALITIES):
        gain = jnp.zeros_like(parts[0])
        for kind, part in zip(kinds, parts):
            gain = gain + jnp.where(kind == m, part, 0.0)
        gain_ref[m * CAP : (m + 1) * CAP, :] = gain
    norm_grad = jnp.dot(spread, rows, preferred_element_type=F32)
    hidden_f = hidden_ref[...].astype(F32)
    inverse = lax.rsqrt(jnp.mean(hidden_f * hidden_f, axis=-1, keepdims=True) + 1e-05)
    normed_f = hidden_f * inverse
    scaled = norm_grad * _gain_rows(labels, gains_ref[...])
    centre = jnp.mean(scaled * normed_f, axis=-1, keepdims=True)
    full = (cot_ref[...].astype(F32) + inverse * (scaled - normed_f * centre)).astype(BF)
    full_ref[...] = full
    width = block_ref.shape[1]
    block_ref[...] = full_ref[:, pl.ds(pl.multiple_of(slot * width, width), width)]
    wide = full.astype(F32)
    count = quarter_ref.shape[0]
    quarter = wide[:count]
    for t in range(1, NS):
        quarter = jnp.where(slot == t, wide[t * count : (t + 1) * count], quarter)
    quarter_ref[...] = quarter.astype(BF)


def finish_norm(slot, kinds, column, hidden, cot, gains, sums, block_width):
    length, width = hidden.shape
    outs = [
        jax.ShapeDtypeStruct((length // NS, width), BF),
        jax.ShapeDtypeStruct((length, block_width), BF),
        jax.ShapeDtypeStruct((MODALITIES * CAP, width // CAP), F32),
    ]
    return pl.pallas_call(
        _finish_kernel,
        grid=(1,),
        in_specs=[SMALL, SMALL] + _whole(column, hidden, cot, gains, *sums),
        out_specs=_whole(*outs),
        out_shape=outs,
        scratch_shapes=[pltpu.VMEM((length, width), BF)],
        compiler_params=_params(),
        cost_estimate=SMALL_COST,
    )(slot, kinds, column, hidden, cot, gains, *sums)


HELD = pl.BlockSpec(memory_space=pltpu.VMEM)


def _load_kernel(w_hbm, out_ref, sem):
    copy = pltpu.make_async_copy(w_hbm.at[0], out_ref, sem)
    copy.start()
    copy.wait()


def load_weight(weight):
    return pl.pallas_call(
        _load_kernel,
        in_specs=[RAW],
        out_specs=HELD,
        out_shape=pltpu.VMEM(weight.shape[1:], weight.dtype),
        scratch_shapes=[pltpu.SemaphoreType.DMA],
        compiler_params=_params(),
        cost_estimate=SMALL_COST,
    )(weight)


def _back_kernel(*refs):
    pieces, w_ref, out_ref = refs[:8], refs[8], refs[9]
    rows = jnp.concatenate([p[...] for p in pieces], axis=0)
    part = _nt(w_ref[...], rows)

    @pl.when(pl.program_id(0) == 0)
    def _():
        out_ref[...] = part

    @pl.when(pl.program_id(0) > 0)
    def _():
        out_ref[...] += part


def back_product(pieces, weight, tile=4096):
    hidden, width = weight.shape[1:]
    rows = sum(p.shape[0] for p in pieces)
    return pl.pallas_call(
        _back_kernel,
        grid=(width // tile,),
        in_specs=[pl.BlockSpec((p.shape[0], tile), lambda i: (0, i)) for p in pieces]
        + [pl.BlockSpec((None, hidden, tile), lambda i: (0, 0, i))],
        out_specs=pl.BlockSpec((hidden, rows), lambda i: (0, 0)),
        out_shape=jax.ShapeDtypeStruct((hidden, rows), F32),
        compiler_params=_params(),
        cost_estimate=SMALL_COST,
    )(*pieces, weight)


CHUNKS = 2
STEP = 1024
OUT_STEP = 2048


def _pre_kernel(*refs):
    pieces, w_ref, back_ref = refs[:8], refs[8], refs[9]
    act_t_ref, grad_t_ref, act_ref, grad_ref, other_hbm = refs[10:15]
    rows_ref, acc_ref, other_ref, sems, out_sems = refs[15:]
    width = w_ref.shape[1]
    size = width // CHUNKS
    part = pieces[0].shape[0]
    copies = []
    for c in range(CHUNKS):
        span = pl.ds(c * size, size)
        group = []
        for p, piece in enumerate(pieces):
            group.append(
                pltpu.make_async_copy(
                    piece.at[:, span], rows_ref.at[pl.ds(p * part, part), span], sems.at[c, p]
                )
            )
        for copy in group:
            copy.start()
        copies.append(group)
    acc_ref[...] = jnp.zeros_like(acc_ref)
    for c in range(CHUNKS):
        for copy in copies[c]:
            copy.wait()

        @pl.loop(0, size // STEP)
        def _(i):
            span = pl.ds(pl.multiple_of(c * size + i * STEP, STEP), STEP)
            acc_ref[...] += _nt(w_ref[:, span], rows_ref[:, span])

    pre = acc_ref[...]
    sigma = jax.nn.sigmoid(pre)
    act = pre * sigma
    grad = back_ref[...] * sigma * (1.0 + pre * (1.0 - sigma))
    grad_t_ref[...] = grad.astype(BF)
    grad_ref[...] = grad.T.astype(BF)
    half = other_ref.shape[0]
    left = grad_ref[half:, :]
    outs = []
    for n in range(width // OUT_STEP):
        span = pl.ds(n * OUT_STEP, OUT_STEP)
        other_ref[:, span] = jnp.dot(left, w_ref[:, span], preferred_element_type=F32).astype(BF)
        copy = pltpu.make_async_copy(other_ref.at[:, span], other_hbm.at[:, span], out_sems.at[n])
        copy.start()
        outs.append(copy)
    act_t_ref[...] = act.astype(BF)
    act_ref[...] = act.T.astype(BF)
    for copy in outs:
        copy.wait()


def pre_product(pieces, weight, back):
    hidden, width = weight.shape
    rows = sum(p.shape[0] for p in pieces)
    outs = (
        [jax.ShapeDtypeStruct((hidden, rows), BF)] * 2
        + [jax.ShapeDtypeStruct((rows, hidden), BF)] * 2
        + [jax.ShapeDtypeStruct((rows // 2, width), BF)]
    )
    return pl.pallas_call(
        _pre_kernel,
        in_specs=[RAW] * 8 + [HELD, HELD],
        out_specs=[HELD] * 4 + [RAW],
        out_shape=outs,
        scratch_shapes=[
            pltpu.VMEM((rows, width), BF),
            pltpu.VMEM((hidden, rows), F32),
            pltpu.VMEM((rows // 2, width), BF),
            pltpu.SemaphoreType.DMA((CHUNKS, 8)),
            pltpu.SemaphoreType.DMA((width // OUT_STEP,)),
        ],
        compiler_params=_params(),
        cost_estimate=SMALL_COST,
    )(*pieces, weight, back)


def _other_kernel(left_ref, w_ref, out_hbm, out_ref, sems):
    half = out_ref.shape[0]
    left = left_ref[half:, :]
    copies = []
    for n in range(out_ref.shape[1] // OUT_STEP):
        span = pl.ds(n * OUT_STEP, OUT_STEP)
        out_ref[:, span] = jnp.dot(left, w_ref[:, span], preferred_element_type=F32).astype(BF)
        copy = pltpu.make_async_copy(out_ref.at[:, span], out_hbm.at[:, span], sems.at[n])
        copy.start()
        copies.append(copy)
    for copy in copies:
        copy.wait()


def other_product(left, weight):
    width = weight.shape[1]
    half = left.shape[0] // 2
    return pl.pallas_call(
        _other_kernel,
        in_specs=[HELD, HELD],
        out_specs=RAW,
        out_shape=jax.ShapeDtypeStruct((half, width), BF),
        scratch_shapes=[pltpu.VMEM((half, width), BF), pltpu.SemaphoreType.DMA((width // OUT_STEP,))],
        compiler_params=_params(),
        cost_estimate=SMALL_COST,
    )(left, weight)


def _split(value):
    high = value.astype(BF)
    return high, (value - high.astype(F32)).astype(BF)


def _own_kernel(count, left_ref, w_ref, in_hbm, *refs):
    rows_hbm, outs_hbm = refs[:count], refs[count : count + 4]
    in_ref, rows_ref, gain_ref = refs[count + 4 : count + 7]
    outs, (sems, out_sems) = refs[count + 7 : count + 11], refs[count + 11 :]
    width = w_ref.shape[1]
    half = in_ref.shape[0]
    part = half // 4
    short = width // part
    groups = []
    for n in range(width // OUT_STEP):
        span = pl.ds(n * OUT_STEP, OUT_STEP)
        group = [pltpu.make_async_copy(in_hbm.at[:, span], in_ref.at[:, span], sems.at[n, 0])]
        for p, piece in enumerate(rows_hbm):
            group.append(
                pltpu.make_async_copy(
                    piece.at[:, span], rows_ref.at[pl.ds(p * part, part), span], sems.at[n, p + 1]
                )
            )
        for copy in group:
            copy.start()
        groups.append(group)
    copies = []

    def put(span, n):
        for k in range(4):
            copy = pltpu.make_async_copy(outs[k].at[:, span], outs_hbm[k].at[:, span], out_sems.at[n, k])
            copy.start()
            copies.append(copy)

    for n, group in enumerate(groups):
        span = pl.ds(n * OUT_STEP, OUT_STEP)
        total = jnp.dot(left_ref[:half, :], w_ref[:, span], preferred_element_type=F32)
        for copy in group:
            copy.wait()
        total = total + in_ref[:, span].astype(F32)
        for k, out_ref in enumerate(outs):
            out_ref[:, span] = total[k * part : (k + 1) * part].astype(out_ref.dtype)
        put(span, n)
        if count:
            gain = jnp.sum(rows_ref[:, span].astype(F32) * total, axis=0, keepdims=True)
            for j in range(OUT_STEP // short):
                row = n * (OUT_STEP // short) + j
                gain_ref[row : row + 1, :] = gain[:, j * short : (j + 1) * short]
    if count:
        high, low = _split(gain_ref[...])
        outs[0][:, width : width + short] = high.astype(F32) + low.astype(F32)
        outs[0][:, width + short :] = jnp.zeros((part, short), F32)
        for out_ref in outs[1:]:
            out_ref[:, width : width + short] = high
            out_ref[:, width + short :] = low
        put(pl.ds(width, 2 * short), len(groups))
    for copy in copies:
        copy.wait()


def own_product(left, weight, arrived, rows=()):
    hidden, width = weight.shape
    half = left.shape[0] // 2
    part = half // 4
    short = width // part
    wide = width + (2 * short if rows else 0)
    kinds = [F32, BF, BF, BF]
    return pl.pallas_call(
        functools.partial(_own_kernel, len(rows)),
        in_specs=[HELD, HELD] + [RAW] * (1 + len(rows)),
        out_specs=[RAW] * 4,
        out_shape=[jax.ShapeDtypeStruct((part, wide), kind) for kind in kinds],
        scratch_shapes=[
            pltpu.VMEM((half, width), BF),
            pltpu.VMEM((half, width) if rows else (16, 128), BF),
            pltpu.VMEM((part, short), F32),
        ]
        + [pltpu.VMEM((part, wide), kind) for kind in kinds]
        + [
            pltpu.SemaphoreType.DMA((width // OUT_STEP, 1 + len(rows))),
            pltpu.SemaphoreType.DMA((width // OUT_STEP + 1, 4)),
        ],
        compiler_params=_params(),
        cost_estimate=SMALL_COST,
    )(left, weight, arrived, *rows)


def _far_norm_kernel(own_ref, *refs):
    arrived, outs = refs[:3], refs[3:]
    part = own_ref.shape[0]
    width = outs[0].shape[1] * CAP // (CAP + 1)
    short = width // part
    total = own_ref[:, :width]
    for ref in arrived:
        total = total + ref[:, :width].astype(F32)
    one, two, three = (
        ref[:, width : width + short].astype(F32) + ref[:, width + short :].astype(F32) for ref in arrived
    )
    gain = (own_ref[:, width : width + short] + two) + (one + three)
    for k, out_ref in enumerate(outs):
        out_ref[:, :width] = total[k * CAP : (k + 1) * CAP]
        for j in range(part // CAP):
            start = width + j * short
            out_ref[:, start : start + short] = gain[j * CAP : (j + 1) * CAP]


def far_norm_sum(pieces, before):
    arrived = [send_stage(pieces[k], False, -k) for k in (1, 2, 3)]
    arrived[0] = after(arrived[0], before)
    part = pieces[0].shape[0]
    width = pieces[0].shape[1] * part // (part + 2)
    outs = [jax.ShapeDtypeStruct((CAP, width + width // CAP), F32)] * 4
    return pl.pallas_call(
        _far_norm_kernel,
        grid=(1,),
        in_specs=_whole(pieces[0], *arrived),
        out_specs=_whole(*outs),
        out_shape=outs,
        compiler_params=_params(),
        cost_estimate=SMALL_COST,
    )(pieces[0], *arrived)


def _near_norm_kernel(*refs):
    zero, one, two, three = (ref[...] for ref in refs[:4])
    out_ref = refs[4]
    width = zero.shape[1] * CAP // (CAP + 1)
    total = (zero + two) + (one + three)
    high, low = _split(total[:, width:])
    out_ref[:, :width] = total[:, :width].astype(BF)
    out_ref[:, width : width + width // CAP] = high
    out_ref[:, width + width // CAP :] = low


def near_norm_sum(blocks, *before):
    arrived = [send_stage(blocks[k], True, -k) for k in (1, 2, 3)]
    arrived[0] = after(arrived[0], *before)
    width = blocks[0].shape[1] * CAP // (CAP + 1)
    out = jax.ShapeDtypeStruct((CAP, width + 2 * (width // CAP)), BF)
    return pl.pallas_call(
        _near_norm_kernel,
        grid=(1,),
        in_specs=_whole(blocks[0], *arrived),
        out_specs=_whole(out)[0],
        out_shape=out,
        compiler_params=_params(),
        cost_estimate=SMALL_COST,
    )(blocks[0], *arrived)


def _near_ffn_kernel(slot_ref, kinds_ref, column_ref, *refs):
    blocks, outs = refs[:4], refs[4:]
    total = blocks[0][...]
    for ref in blocks[1:]:
        total = total + ref[...].astype(F32)
    slot = slot_ref[0]
    spreader = _slot_spreader(column_ref[...], kinds_ref[slot])
    length = spreader.shape[0]
    part = length // NS
    row = lax.broadcasted_iota(jnp.int32, (length, length), 0)
    token = lax.broadcasted_iota(jnp.int32, (length, length), 1)
    turned = jnp.where(token == lax.rem(row + slot * part, length), 1.0, 0.0)
    turned = jnp.dot(turned, spreader, preferred_element_type=F32).astype(BF)
    rows = jnp.dot(turned, total.astype(BF), preferred_element_type=F32)
    for k, out_ref in enumerate(outs):
        out_ref[...] = rows[k * part : (k + 1) * part].astype(BF)


def near_ffn_sum(slot, kinds, column, total, before):
    blocks = [total[k * CAP : (k + 1) * CAP] for k in range(4)]
    arrived = [send_stage(blocks[k].astype(BF), True, -k) for k in (1, 2, 3)]
    arrived[0] = after(arrived[0], before)
    outs = [jax.ShapeDtypeStruct((column.shape[0] // NS, total.shape[1]), BF)] * NS
    return pl.pallas_call(
        _near_ffn_kernel,
        grid=(1,),
        in_specs=[SMALL, SMALL] + _whole(column, blocks[0], *arrived),
        out_specs=_whole(*outs),
        out_shape=outs,
        compiler_params=_params(),
        cost_estimate=SMALL_COST,
    )(slot, kinds, column, blocks[0], *arrived)


def _down_kernel(*refs):
    left_ref, out_ref = refs[8:]
    rows = jnp.concatenate([p[...] for p in refs[:8]], axis=0)
    out_ref[...] = jnp.dot(left_ref[...], rows, preferred_element_type=F32).astype(BF)


def weight_grad(pieces, left, shape, tile=4096):
    _, hidden, width = shape
    count = left.shape[1]
    weight_spec = pl.BlockSpec((None, hidden, tile), lambda i: (0, 0, i))
    return pl.pallas_call(
        _down_kernel,
        grid=(width // tile,),
        in_specs=[pl.BlockSpec((p.shape[0], tile), lambda i: (0, i)) for p in pieces]
        + [pl.BlockSpec((hidden, count), lambda i: (0, 0))],
        out_specs=weight_spec,
        out_shape=jax.ShapeDtypeStruct(shape, BF),
        compiler_params=_params(),
        cost_estimate=pl.CostEstimate(
            flops=2 * hidden * count * width,
            bytes_accessed=2 * width * (hidden + count),
            transcendentals=0,
        ),
    )(*pieces, left)


def after(value, *others):
    return lax.optimization_barrier((value, *others))[0]


def on_device(
    queries, keys, values, residual, labels, slot_modality, gains, up_weight, down_weight, cotangent
):
    slot_index = lax.axis_index("sect")
    slot = slot_index.astype(jnp.int32).reshape(1)
    column = labels.reshape(-1, 1)
    length = labels.shape[1]
    grad_full = cotangent[0]
    packed_cot = pack_rows(slot, slot_modality, labels, grad_full)
    queries, keys, values, _ = lax.optimization_barrier((queries, keys, values, packed_cot))
    cot_near = gather_near(packed_cot)

    attended_block, probs, probs_b = causal_forward(queries, keys, values)
    block = attended_block[0]
    blocks = [block] + [send_sect(block, k) for k in (1, 2, 3)]
    hidden, packed = norm_rows_of(
        slot, slot_modality, labels, column, after(residual[0], cot_near), gains, blocks
    )
    cot_far = gather_far(cot_near)
    cot_rows = cot_far + [swap_core(piece) for piece in cot_far]
    near = gather_near(after(packed, *cot_far[1:]))
    far = gather_far(near)
    back = back_product(cot_rows, down_weight)
    up_held = load_weight(up_weight)
    down_held = load_weight(down_weight)
    far[3] = after(far[3], back, up_held, down_held)
    token_rows = far + [swap_core(piece) for piece in far]

    act_t, grad_t, act, grad, norm_other = pre_product(token_rows, up_held, back)
    norm_arrived = swap_core(norm_other)
    ffn_other = other_product(after(act, norm_other), down_held)
    ffn_arrived = swap_core(ffn_other)
    norm_pieces = own_product(after(grad, ffn_other), up_held, norm_arrived, far)
    ffn_pieces = own_product(after(act, norm_pieces[0]), down_held, ffn_arrived)
    down_grad = weight_grad(cot_rows, after(act_t, ffn_pieces[0]), up_weight.shape)
    norm_blocks = far_norm_sum(norm_pieces, down_grad)
    up_grad = weight_grad(token_rows, after(grad_t, norm_blocks[0]), up_weight.shape)
    ffn_arrived = [send_stage(ffn_pieces[k], False, -k) for k in (1, 2, 3)]
    norm_rows = near_norm_sum(norm_blocks, up_grad, *ffn_arrived)
    ffn_total = after(ffn_pieces[0], norm_rows) + sum(piece.astype(F32) for piece in ffn_arrived)
    sums = [norm_rows] + [send_sect(norm_rows, k) for k in (1, 2, 3)]
    residual_grad, grad_block, gain_part = finish_norm(
        slot, slot_modality, column, hidden, grad_full, gains, sums, queries.shape[2]
    )
    parts = near_ffn_sum(slot, slot_modality, column, ffn_total, grad_block)
    query_grad, key_grad, value_grad = causal_backward(
        after(grad_block, parts[0])[None], queries, keys, values, attended_block, probs, probs_b
    )

    gain_sum = gain_part + swap_core(gain_part)
    width = hidden.shape[1]
    gain_sum = gain_sum.reshape(MODALITIES, CAP, 4, -1).transpose(0, 2, 1, 3).reshape(MODALITIES, width)
    gain_grad = gain_sum / gains

    quarter = length // NS
    total = parts[0].astype(F32)
    for k in (1, 2, 3):
        total = total + send_sect(parts[k], k).astype(F32)
    hidden_q = lax.dynamic_slice_in_dim(hidden, slot_index * quarter, quarter, 0)
    output = (hidden_q.astype(F32) + total).astype(BF)[None]
    return (
        output,
        residual_grad[None],
        query_grad,
        key_grad,
        value_grad,
        up_grad,
        down_grad,
        gain_grad,
    )


def solution(mesh):
    in_specs = (
        P("dp", None, "sect"),
        P("dp", None, "sect"),
        P("dp", None, "sect"),
        P("dp", None, None),
        P("dp", None),
        P(),
        P(),
        P("sect", "dp", None),
        P("sect", "dp", None),
        P("dp", None, None),
    )
    out_specs = (
        P("dp", "sect", None),
        P("dp", "sect", None),
        P("dp", None, "sect"),
        P("dp", None, "sect"),
        P("dp", None, "sect"),
        P("sect", "dp", None),
        P("sect", "dp", None),
        P(),
    )
    return jax.shard_map(
        on_device, mesh=mesh, in_specs=in_specs, out_specs=out_specs, check_vma=False
    )
```

```python
import functools

import jax
import jax.numpy as jnp
from jax import lax
from jax.experimental import pallas as pl
from jax.experimental.pallas import tpu as pltpu
from jax.sharding import PartitionSpec as P

HD = 128
MODALITIES = 3
NZ = 4
NX = 4
NC = 2
NS = 4
AXES = ("dp", "sect")
BF = jnp.bfloat16
F32 = jnp.float32
CAP = 8
VMEM = 26 * 1024 * 1024


def causal_forward(queries, keys, values):
    seq_count, length, width = queries.shape
    head_count = width // HD
    query_f = queries.astype(F32).reshape(seq_count, length, head_count, HD)
    key_f = keys.astype(F32).reshape(seq_count, length, head_count, HD)
    value_f = values.astype(F32).reshape(seq_count, length, head_count, HD)
    scores = jnp.einsum("sqhd,skhd->shqk", query_f, key_f) * HD ** (-0.5)
    position = jnp.arange(length)
    causal = position[:, None] >= position[None, :]
    scores = jnp.where(causal, scores, -1e30)
    probs = jax.nn.softmax(scores, axis=-1)
    probs_b = probs.astype(BF)
    attended = jnp.einsum("shqk,skhd->sqhd", probs_b.astype(F32), value_f)
    return (attended.astype(BF).reshape(seq_count, length, width), probs, probs_b)


def causal_backward(grad_out, queries, keys, values, attended, probs, probs_b):
    seq_count, length, width = queries.shape
    head_count = width // HD
    shape = (seq_count, length, head_count, HD)
    grad_f = grad_out.astype(F32).reshape(shape)
    query_f = queries.astype(F32).reshape(shape)
    key_f = keys.astype(F32).reshape(shape)
    value_f = values.astype(F32).reshape(shape)
    attended_f = attended.astype(F32).reshape(shape)
    value_grad = jnp.einsum("shqk,sqhd->skhd", probs_b.astype(F32), grad_f).astype(BF)
    dprob = jnp.einsum("sqhd,skhd->shqk", grad_f, value_f)
    delta = jnp.einsum("sqhd,sqhd->shq", grad_f, attended_f)
    dscore = (probs * (dprob - delta[..., None]) * HD ** (-0.5)).astype(BF).astype(F32)
    query_grad = jnp.einsum("shqk,skhd->sqhd", dscore, key_f).astype(BF)
    key_grad = jnp.einsum("shqk,sqhd->skhd", dscore, query_f).astype(BF)
    return (
        query_grad.reshape(seq_count, length, width),
        key_grad.reshape(seq_count, length, width),
        value_grad.reshape(seq_count, length, width),
    )


def _pairs(move):
    out = []
    for z in range(NZ):
        for x in range(NX):
            for c in range(NC):
                for s in range(NS):
                    z2, x2, c2, s2 = move(z, x, c, s)
                    source = ((z * NX + x) * NC + c) * NS + s
                    target = (((z2 % NZ) * NX + x2 % NX) * NC + c2) * NS + s2 % NS
                    out.append((source, target))
    return out


def along(first, shift):
    def move(z, x, c, s):
        if (c == 0) == first:
            return z, x + shift, c, s
        return z + shift, x, c, s

    return _pairs(move)


def send(block, pairs):
    return lax.ppermute(block, AXES, pairs)


def send_stage(block, first, shift):
    return send(block, along(first, shift))


def swap_core(block):
    return send(block, _pairs(lambda z, x, c, s: (z, x, 1 - c, s)))


def send_sect(block, shift):
    return send(block, _pairs(lambda z, x, c, s: (z, x, c, s + shift)))


def gather_near(block):
    return jnp.concatenate([block] + [send_stage(block, True, k) for k in (1, 2, 3)], axis=0)


def gather_far(near):
    return [near] + [send_stage(near, False, k) for k in (1, 2, 3)]


def _params(limit=VMEM):
    return pltpu.CompilerParams(vmem_limit_bytes=limit)


def _nt(left, right):
    return lax.dot_general(left, right, (((1,), (1,)), ((), ())), preferred_element_type=F32)


def _slot_selector(labels, kind):
    length = labels.shape[1]
    keep = jnp.broadcast_to((labels == kind).astype(F32), (CAP, length))
    first = lax.broadcasted_iota(jnp.int32, (length, length), 0)
    second = lax.broadcasted_iota(jnp.int32, (length, length), 1)
    rank = jnp.dot(keep, (first <= second).astype(F32), preferred_element_type=F32)
    row = lax.broadcasted_iota(jnp.int32, (CAP, length), 0).astype(F32)
    return jnp.where((rank == row + 1.0) & (keep > 0.5), 1.0, 0.0)


def _slot_spreader(labels, kind):
    length = labels.shape[0]
    keep = jnp.broadcast_to((labels == kind.astype(F32)).astype(F32), (length, CAP))
    first = lax.broadcasted_iota(jnp.int32, (length, length), 0)
    second = lax.broadcasted_iota(jnp.int32, (length, length), 1)
    rank = jnp.dot((second <= first).astype(F32), keep, preferred_element_type=F32)
    column = lax.broadcasted_iota(jnp.int32, (length, CAP), 1).astype(F32)
    return jnp.where((rank == column + 1.0) & (keep > 0.5), 1.0, 0.0)


SMALL_COST = pl.CostEstimate(flops=1000, bytes_accessed=1000, transcendentals=0)
SMALL = pl.BlockSpec(memory_space=pltpu.SMEM)
def _whole(*arrays):
    return [pl.BlockSpec(a.shape, lambda i, n=len(a.shape): (0,) * n) for a in arrays]


RAW = pl.BlockSpec(memory_space=pl.ANY)
HELD = pl.BlockSpec(memory_space=pltpu.VMEM)


def _pack_kernel(slot_ref, kinds_hbm, labels_hbm, rows_hbm, out_ref, select_ref, column_ref, *refs):
    kinds_ref, labels_ref, rows_ref, sems = refs
    copies = [
        pltpu.make_async_copy(kinds_hbm, kinds_ref, sems.at[0]),
        pltpu.make_async_copy(labels_hbm, labels_ref, sems.at[1]),
        pltpu.make_async_copy(rows_hbm, rows_ref, sems.at[2]),
    ]
    for copy in copies:
        copy.start()
    copies[0].wait()
    copies[1].wait()
    labels = labels_ref[...]
    length = labels.shape[1]
    select = _slot_selector(labels, kinds_ref[slot_ref[0]]).astype(BF)
    select_ref[...] = select
    first = lax.broadcasted_iota(jnp.int32, (length, length), 0)
    second = lax.broadcasted_iota(jnp.int32, (length, length), 1)
    spread = jnp.where(first == second, jnp.broadcast_to(labels, (length, length)), 0)
    column_ref[...] = jnp.sum(spread.astype(F32), axis=1, keepdims=True)
    copies[2].wait()
    out_ref[...] = jnp.dot(select, rows_ref[...], preferred_element_type=F32).astype(BF)


def pack_rows(slot, kinds, labels, rows):
    length, width = rows.shape
    outs = [
        jax.ShapeDtypeStruct((CAP, width), BF),
        jax.ShapeDtypeStruct((CAP, length), BF),
        jax.ShapeDtypeStruct((length, 1), F32),
    ]
    return pl.pallas_call(
        _pack_kernel,
        in_specs=[SMALL, RAW, RAW, RAW],
        out_specs=[HELD] * 3,
        out_shape=outs,
        scratch_shapes=[
            pltpu.SMEM(kinds.shape, jnp.int32),
            pltpu.VMEM(labels.shape, jnp.int32),
            pltpu.VMEM(rows.shape, BF),
            pltpu.SemaphoreType.DMA((3,)),
        ],
        compiler_params=_params(),
        cost_estimate=SMALL_COST,
    )(slot, kinds, labels, rows)


def _gain_rows(labels, gains):
    return jnp.where(labels == 0.0, gains[0:1], jnp.where(labels == 1.0, gains[1:2], gains[2:3]))


def _norm_kernel(slot_ref, select_ref, column_ref, residual_hbm, gains_hbm, *refs):
    blocks, (hidden_ref, packed_ref, joined_ref, residual_ref, gains_ref, sems) = refs[:NS], refs[NS:]
    copies = [
        pltpu.make_async_copy(residual_hbm, residual_ref, sems.at[0]),
        pltpu.make_async_copy(gains_hbm, gains_ref, sems.at[1]),
    ]
    for copy in copies:
        copy.start()
    slot = slot_ref[0]
    width = blocks[0].shape[1]
    for k, block in enumerate(blocks):
        owner = lax.rem(slot - k + NS, NS)
        joined_ref[:, pl.ds(pl.multiple_of(owner * width, width), width)] = block[...]
    for copy in copies:
        copy.wait()
    hidden = (residual_ref[...].astype(F32) + joined_ref[...].astype(F32)).astype(BF)
    hidden_ref[...] = hidden
    hidden_f = hidden.astype(F32)
    inverse = lax.rsqrt(jnp.mean(hidden_f * hidden_f, axis=-1, keepdims=True) + 1e-05)
    normed = (hidden_f * inverse * _gain_rows(column_ref[...], gains_ref[...])).astype(BF)
    packed_ref[...] = jnp.dot(select_ref[...], normed, preferred_element_type=F32).astype(BF)


def norm_rows_of(slot, select, column, residual, gains, blocks):
    length, width = residual.shape
    outs = [jax.ShapeDtypeStruct((length, width), BF), jax.ShapeDtypeStruct((CAP, width), BF)]
    return pl.pallas_call(
        _norm_kernel,
        in_specs=[SMALL, HELD, HELD, RAW, RAW] + [HELD] * NS,
        out_specs=[HELD, HELD],
        out_shape=outs,
        scratch_shapes=[
            pltpu.VMEM((length, width), BF),
            pltpu.VMEM((length, width), BF),
            pltpu.VMEM(gains.shape, F32),
            pltpu.SemaphoreType.DMA((2,)),
        ],
        compiler_params=_params(),
        cost_estimate=SMALL_COST,
    )(slot, select, column, residual, gains, *blocks)


def _finish_kernel(slot_ref, kinds_ref, column_ref, hidden_ref, cot_ref, gains_ref, *refs):
    sums, (quarter_ref, block_ref, gain_ref, full_ref) = refs[:NS], refs[NS:]
    slot = slot_ref[0]
    labels = column_ref[...]
    kinds = [kinds_ref[lax.rem(slot - k + NS, NS)] for k in range(NS)]
    spreaders = [_slot_spreader(labels, kind) for kind in kinds]
    spread = jnp.concatenate(spreaders, axis=1).astype(BF)
    wide = hidden_ref.shape[1]
    rows = jnp.concatenate([s[:, :wide].astype(F32) for s in sums], axis=0).astype(BF)
    extra = wide // CAP
    parts = [
        s[:, wide : wide + extra].astype(F32) + s[:, wide + extra :].astype(F32) for s in sums
    ]
    for m in range(MODALITIES):
        gain = jnp.zeros_like(parts[0])
        for kind, part in zip(kinds, parts):
            gain = gain + jnp.where(kind == m, part, 0.0)
        gain_ref[m * CAP : (m + 1) * CAP, :] = gain
    norm_grad = jnp.dot(spread, rows, preferred_element_type=F32)
    hidden_f = hidden_ref[...].astype(F32)
    inverse = lax.rsqrt(jnp.mean(hidden_f * hidden_f, axis=-1, keepdims=True) + 1e-05)
    normed_f = hidden_f * inverse
    scaled = norm_grad * _gain_rows(labels, gains_ref[...])
    centre = jnp.mean(scaled * normed_f, axis=-1, keepdims=True)
    full = (cot_ref[...].astype(F32) + inverse * (scaled - normed_f * centre)).astype(BF)
    full_ref[...] = full
    width = block_ref.shape[1]
    block_ref[...] = full_ref[:, pl.ds(pl.multiple_of(slot * width, width), width)]
    wide = full.astype(F32)
    count = quarter_ref.shape[0]
    quarter = wide[:count]
    for t in range(1, NS):
        quarter = jnp.where(slot == t, wide[t * count : (t + 1) * count], quarter)
    quarter_ref[...] = quarter.astype(BF)


def finish_norm(slot, kinds, column, hidden, cot, gains, sums, block_width):
    length, width = hidden.shape
    outs = [
        jax.ShapeDtypeStruct((length // NS, width), BF),
        jax.ShapeDtypeStruct((length, block_width), BF),
        jax.ShapeDtypeStruct((MODALITIES * CAP, width // CAP), F32),
    ]
    return pl.pallas_call(
        _finish_kernel,
        grid=(1,),
        in_specs=[SMALL, SMALL] + _whole(column, hidden, cot, gains, *sums),
        out_specs=_whole(*outs),
        out_shape=outs,
        scratch_shapes=[pltpu.VMEM((length, width), BF)],
        compiler_params=_params(),
        cost_estimate=SMALL_COST,
    )(slot, kinds, column, hidden, cot, gains, *sums)


def _load_kernel(w_hbm, out_ref, sem):
    copy = pltpu.make_async_copy(w_hbm.at[0], out_ref, sem)
    copy.start()
    copy.wait()


def load_weight(weight):
    return pl.pallas_call(
        _load_kernel,
        in_specs=[RAW],
        out_specs=HELD,
        out_shape=pltpu.VMEM(weight.shape[1:], weight.dtype),
        scratch_shapes=[pltpu.SemaphoreType.DMA],
        compiler_params=_params(),
        cost_estimate=SMALL_COST,
    )(weight)


def _back_kernel(*refs):
    pieces, w_ref, out_ref = refs[:8], refs[8], refs[9]
    rows = jnp.concatenate([p[...] for p in pieces], axis=0)
    part = _nt(w_ref[...], rows)

    @pl.when(pl.program_id(0) == 0)
    def _():
        out_ref[...] = part

    @pl.when(pl.program_id(0) > 0)
    def _():
        out_ref[...] += part


def back_product(pieces, weight, tile=4096):
    hidden, width = weight.shape[1:]
    rows = sum(p.shape[0] for p in pieces)
    return pl.pallas_call(
        _back_kernel,
        grid=(width // tile,),
        in_specs=[pl.BlockSpec((p.shape[0], tile), lambda i: (0, i)) for p in pieces]
        + [pl.BlockSpec((None, hidden, tile), lambda i: (0, 0, i))],
        out_specs=pl.BlockSpec((hidden, rows), lambda i: (0, 0)),
        out_shape=jax.ShapeDtypeStruct((hidden, rows), F32),
        compiler_params=_params(),
        cost_estimate=SMALL_COST,
    )(*pieces, weight)


CHUNKS = 2
STEP = 1024
OUT_STEP = 2048


def _pre_kernel(*refs):
    pieces, w_ref, back_ref = refs[:8], refs[8], refs[9]
    act_t_ref, grad_t_ref, act_ref, grad_ref, other_hbm = refs[10:15]
    rows_ref, acc_ref, other_ref, sems, out_sems = refs[15:]
    width = w_ref.shape[1]
    size = width // CHUNKS
    part = pieces[0].shape[0]
    copies = []
    for c in range(CHUNKS):
        span = pl.ds(c * size, size)
        group = []
        for p, piece in enumerate(pieces):
            group.append(
                pltpu.make_async_copy(
                    piece.at[:, span], rows_ref.at[pl.ds(p * part, part), span], sems.at[c, p]
                )
            )
        for copy in group:
            copy.start()
        copies.append(group)
    acc_ref[...] = jnp.zeros_like(acc_ref)
    for c in range(CHUNKS):
        for copy in copies[c]:
            copy.wait()

        @pl.loop(0, size // STEP)
        def _(i):
            span = pl.ds(pl.multiple_of(c * size + i * STEP, STEP), STEP)
            acc_ref[...] += _nt(w_ref[:, span], rows_ref[:, span])

    pre = acc_ref[...]
    sigma = jax.nn.sigmoid(pre)
    act = pre * sigma
    grad = back_ref[...] * sigma * (1.0 + pre * (1.0 - sigma))
    grad_t_ref[...] = grad.astype(BF)
    grad_ref[...] = grad.T.astype(BF)
    half = other_ref.shape[0]
    left = grad_ref[half:, :]
    outs = []
    for n in range(width // OUT_STEP):
        span = pl.ds(n * OUT_STEP, OUT_STEP)
        other_ref[:, span] = jnp.dot(left, w_ref[:, span], preferred_element_type=F32).astype(BF)
        copy = pltpu.make_async_copy(other_ref.at[:, span], other_hbm.at[:, span], out_sems.at[n])
        copy.start()
        outs.append(copy)
    act_t_ref[...] = act.astype(BF)
    act_ref[...] = act.T.astype(BF)
    for copy in outs:
        copy.wait()


def pre_product(pieces, weight, back):
    hidden, width = weight.shape
    rows = sum(p.shape[0] for p in pieces)
    outs = (
        [jax.ShapeDtypeStruct((hidden, rows), BF)] * 2
        + [jax.ShapeDtypeStruct((rows, hidden), BF)] * 2
        + [jax.ShapeDtypeStruct((rows // 2, width), BF)]
    )
    return pl.pallas_call(
        _pre_kernel,
        in_specs=[RAW] * 8 + [HELD, HELD],
        out_specs=[HELD] * 4 + [RAW],
        out_shape=outs,
        scratch_shapes=[
            pltpu.VMEM((rows, width), BF),
            pltpu.VMEM((hidden, rows), F32),
            pltpu.VMEM((rows // 2, width), BF),
            pltpu.SemaphoreType.DMA((CHUNKS, 8)),
            pltpu.SemaphoreType.DMA((width // OUT_STEP,)),
        ],
        compiler_params=_params(),
        cost_estimate=SMALL_COST,
    )(*pieces, weight, back)


def _other_kernel(left_ref, w_ref, out_hbm, out_ref, sems):
    half = out_ref.shape[0]
    left = left_ref[half:, :]
    copies = []
    for n in range(out_ref.shape[1] // OUT_STEP):
        span = pl.ds(n * OUT_STEP, OUT_STEP)
        out_ref[:, span] = jnp.dot(left, w_ref[:, span], preferred_element_type=F32).astype(BF)
        copy = pltpu.make_async_copy(out_ref.at[:, span], out_hbm.at[:, span], sems.at[n])
        copy.start()
        copies.append(copy)
    for copy in copies:
        copy.wait()


def other_product(left, weight):
    width = weight.shape[1]
    half = left.shape[0] // 2
    return pl.pallas_call(
        _other_kernel,
        in_specs=[HELD, HELD],
        out_specs=RAW,
        out_shape=jax.ShapeDtypeStruct((half, width), BF),
        scratch_shapes=[pltpu.VMEM((half, width), BF), pltpu.SemaphoreType.DMA((width // OUT_STEP,))],
        compiler_params=_params(),
        cost_estimate=SMALL_COST,
    )(left, weight)


def _split(value):
    high = value.astype(BF)
    return high, (value - high.astype(F32)).astype(BF)


def _own_kernel(count, left_ref, w_ref, in_ref, *refs):
    rows_hbm, outs = refs[:count], refs[count : count + 4]
    rows_ref, gain_ref, sems = refs[count + 4 :]
    width = w_ref.shape[1]
    half = in_ref.shape[0]
    part = half // 4
    short = width // part
    groups = []
    for n in range(width // OUT_STEP):
        span = pl.ds(n * OUT_STEP, OUT_STEP)
        group = [
            pltpu.make_async_copy(piece.at[:, span], rows_ref.at[pl.ds(p * part, part), span], sems.at[n, p])
            for p, piece in enumerate(rows_hbm)
        ]
        for copy in group:
            copy.start()
        groups.append(group)
    for n, group in enumerate(groups):
        span = pl.ds(n * OUT_STEP, OUT_STEP)
        total = jnp.dot(left_ref[:half, :], w_ref[:, span], preferred_element_type=F32)
        total = total + in_ref[:, span].astype(F32)
        for k, out_ref in enumerate(outs):
            out_ref[:, span] = total[k * part : (k + 1) * part].astype(out_ref.dtype)
        if count:
            for copy in group:
                copy.wait()
            gain = jnp.sum(rows_ref[:, span].astype(F32) * total, axis=0, keepdims=True)
            for j in range(OUT_STEP // short):
                row = n * (OUT_STEP // short) + j
                gain_ref[row : row + 1, :] = gain[:, j * short : (j + 1) * short]
    if count:
        high, low = _split(gain_ref[...])
        outs[0][:, width : width + short] = high.astype(F32) + low.astype(F32)
        outs[0][:, width + short :] = jnp.zeros((part, short), F32)
        for out_ref in outs[1:]:
            out_ref[:, width : width + short] = high
            out_ref[:, width + short :] = low


def own_product(left, weight, arrived, rows=()):
    hidden, width = weight.shape
    half = left.shape[0] // 2
    part = half // 4
    short = width // part
    wide = width + (2 * short if rows else 0)
    kinds = [F32, BF, BF, BF]
    return pl.pallas_call(
        functools.partial(_own_kernel, len(rows)),
        in_specs=[HELD, HELD, HELD] + [RAW] * len(rows),
        out_specs=[HELD] * 4,
        out_shape=[jax.ShapeDtypeStruct((part, wide), kind) for kind in kinds],
        scratch_shapes=[
            pltpu.VMEM((half, width) if rows else (16, 128), BF),
            pltpu.VMEM((part, short), F32),
            pltpu.SemaphoreType.DMA((width // OUT_STEP, max(1, len(rows)))),
        ],
        compiler_params=_params(),
        cost_estimate=SMALL_COST,
    )(left, weight, arrived, *rows)


def _far_norm_kernel(own_ref, *refs):
    arrived, outs = refs[:3], refs[3:]
    part = own_ref.shape[0]
    width = outs[0].shape[1] * CAP // (CAP + 1)
    short = width // part
    total = own_ref[:, :width]
    for ref in arrived:
        total = total + ref[:, :width].astype(F32)
    one, two, three = (
        ref[:, width : width + short].astype(F32) + ref[:, width + short :].astype(F32) for ref in arrived
    )
    gain = (own_ref[:, width : width + short] + two) + (one + three)
    for k, out_ref in enumerate(outs):
        out_ref[:, :width] = total[k * CAP : (k + 1) * CAP]
        for j in range(part // CAP):
            start = width + j * short
            out_ref[:, start : start + short] = gain[j * CAP : (j + 1) * CAP]


def far_norm_sum(pieces, before):
    arrived = [send_stage(pieces[k], False, -k) for k in (1, 2, 3)]
    arrived[0] = after(arrived[0], before)
    part = pieces[0].shape[0]
    width = pieces[0].shape[1] * part // (part + 2)
    outs = [jax.ShapeDtypeStruct((CAP, width + width // CAP), F32)] * 4
    return pl.pallas_call(
        _far_norm_kernel,
        grid=(1,),
        in_specs=_whole(pieces[0], *arrived),
        out_specs=_whole(*outs),
        out_shape=outs,
        compiler_params=_params(),
        cost_estimate=SMALL_COST,
    )(pieces[0], *arrived)


def _near_norm_kernel(*refs):
    zero, one, two, three = (ref[...] for ref in refs[:4])
    out_ref = refs[4]
    width = zero.shape[1] * CAP // (CAP + 1)
    total = (zero + two) + (one + three)
    high, low = _split(total[:, width:])
    out_ref[:, :width] = total[:, :width].astype(BF)
    out_ref[:, width : width + width // CAP] = high
    out_ref[:, width + width // CAP :] = low


def near_norm_sum(blocks, *before):
    arrived = [send_stage(blocks[k], True, -k) for k in (1, 2, 3)]
    arrived[0] = after(arrived[0], *before)
    width = blocks[0].shape[1] * CAP // (CAP + 1)
    out = jax.ShapeDtypeStruct((CAP, width + 2 * (width // CAP)), BF)
    return pl.pallas_call(
        _near_norm_kernel,
        grid=(1,),
        in_specs=_whole(blocks[0], *arrived),
        out_specs=_whole(out)[0],
        out_shape=out,
        compiler_params=_params(),
        cost_estimate=SMALL_COST,
    )(blocks[0], *arrived)


def _near_ffn_kernel(slot_ref, kinds_ref, column_ref, *refs):
    blocks, outs = refs[:4], refs[4:]
    total = blocks[0][...]
    for ref in blocks[1:]:
        total = total + ref[...].astype(F32)
    slot = slot_ref[0]
    spreader = _slot_spreader(column_ref[...], kinds_ref[slot])
    length = spreader.shape[0]
    part = length // NS
    row = lax.broadcasted_iota(jnp.int32, (length, length), 0)
    token = lax.broadcasted_iota(jnp.int32, (length, length), 1)
    turned = jnp.where(token == lax.rem(row + slot * part, length), 1.0, 0.0)
    turned = jnp.dot(turned, spreader, preferred_element_type=F32).astype(BF)
    rows = jnp.dot(turned, total.astype(BF), preferred_element_type=F32)
    for k, out_ref in enumerate(outs):
        out_ref[...] = rows[k * part : (k + 1) * part].astype(BF)


def near_ffn_sum(slot, kinds, column, total, before):
    blocks = [total[k * CAP : (k + 1) * CAP] for k in range(4)]
    arrived = [send_stage(blocks[k].astype(BF), True, -k) for k in (1, 2, 3)]
    arrived[0] = after(arrived[0], before)
    outs = [jax.ShapeDtypeStruct((column.shape[0] // NS, total.shape[1]), BF)] * NS
    return pl.pallas_call(
        _near_ffn_kernel,
        grid=(1,),
        in_specs=[SMALL, SMALL] + _whole(column, blocks[0], *arrived),
        out_specs=_whole(*outs),
        out_shape=outs,
        compiler_params=_params(),
        cost_estimate=SMALL_COST,
    )(slot, kinds, column, blocks[0], *arrived)


def _down_kernel(*refs):
    left_ref, out_ref = refs[8:]
    rows = jnp.concatenate([p[...] for p in refs[:8]], axis=0)
    out_ref[...] = jnp.dot(left_ref[...], rows, preferred_element_type=F32).astype(BF)


def weight_grad(pieces, left, shape, tile=4096):
    _, hidden, width = shape
    count = left.shape[1]
    weight_spec = pl.BlockSpec((None, hidden, tile), lambda i: (0, 0, i))
    return pl.pallas_call(
        _down_kernel,
        grid=(width // tile,),
        in_specs=[pl.BlockSpec((p.shape[0], tile), lambda i: (0, i)) for p in pieces]
        + [pl.BlockSpec((hidden, count), lambda i: (0, 0))],
        out_specs=weight_spec,
        out_shape=jax.ShapeDtypeStruct(shape, BF),
        compiler_params=_params(),
        cost_estimate=pl.CostEstimate(
            flops=2 * hidden * count * width,
            bytes_accessed=2 * width * (hidden + count),
            transcendentals=0,
        ),
    )(*pieces, left)


def after(value, *others):
    return lax.optimization_barrier((value, *others))[0]


def on_device(
    queries, keys, values, residual, labels, slot_modality, gains, up_weight, down_weight, cotangent
):
    slot_index = lax.axis_index("sect")
    slot = slot_index.astype(jnp.int32).reshape(1)
    length = labels.shape[1]
    grad_full = cotangent[0]
    packed_cot, select, column = pack_rows(slot, slot_modality, labels, grad_full)
    queries, keys, values, _ = lax.optimization_barrier((queries, keys, values, packed_cot))
    cot_near = gather_near(packed_cot)

    attended_block, probs, probs_b = causal_forward(queries, keys, values)
    block = attended_block[0]
    blocks = [block] + [send_sect(block, k) for k in (1, 2, 3)]
    hidden, packed = norm_rows_of(slot, after(select, cot_near), column, residual[0], gains, blocks)
    cot_far = gather_far(cot_near)
    cot_rows = cot_far + [swap_core(piece) for piece in cot_far]
    near = gather_near(after(packed, *cot_far[1:]))
    far = gather_far(near)
    back = back_product(cot_rows, down_weight)
    up_held = load_weight(up_weight)
    down_held = load_weight(down_weight)
    far[3] = after(far[3], back, up_held, down_held)
    token_rows = far + [swap_core(piece) for piece in far]

    act_t, grad_t, act, grad, norm_other = pre_product(token_rows, up_held, back)
    norm_arrived = swap_core(norm_other)
    ffn_other = other_product(after(act, norm_other), down_held)
    ffn_arrived = swap_core(ffn_other)
    norm_pieces = own_product(after(grad, ffn_other), up_held, norm_arrived, far)
    ffn_pieces = own_product(after(act, norm_pieces[0]), down_held, ffn_arrived)
    down_grad = weight_grad(cot_rows, after(act_t, ffn_pieces[0]), up_weight.shape)
    norm_blocks = far_norm_sum(norm_pieces, down_grad)
    up_grad = weight_grad(token_rows, after(grad_t, norm_blocks[0]), up_weight.shape)
    ffn_arrived = [send_stage(ffn_pieces[k], False, -k) for k in (1, 2, 3)]
    norm_rows = near_norm_sum(norm_blocks, up_grad, *ffn_arrived)
    ffn_total = after(ffn_pieces[0], norm_rows) + sum(piece.astype(F32) for piece in ffn_arrived)
    sums = [norm_rows] + [send_sect(norm_rows, k) for k in (1, 2, 3)]
    residual_grad, grad_block, gain_part = finish_norm(
        slot, slot_modality, column, hidden, grad_full, gains, sums, queries.shape[2]
    )
    parts = near_ffn_sum(slot, slot_modality, column, ffn_total, grad_block)
    query_grad, key_grad, value_grad = causal_backward(
        after(grad_block, parts[0])[None], queries, keys, values, attended_block, probs, probs_b
    )

    gain_sum = gain_part + swap_core(gain_part)
    width = hidden.shape[1]
    gain_sum = gain_sum.reshape(MODALITIES, CAP, 4, -1).transpose(0, 2, 1, 3).reshape(MODALITIES, width)
    gain_grad = gain_sum / gains

    quarter = length // NS
    total = parts[0].astype(F32)
    for k in (1, 2, 3):
        total = total + send_sect(parts[k], k).astype(F32)
    hidden_q = lax.dynamic_slice_in_dim(hidden, slot_index * quarter, quarter, 0)
    output = (hidden_q.astype(F32) + total).astype(BF)[None]
    return (
        output,
        residual_grad[None],
        query_grad,
        key_grad,
        value_grad,
        up_grad,
        down_grad,
        gain_grad,
    )


def solution(mesh):
    in_specs = (
        P("dp", None, "sect"),
        P("dp", None, "sect"),
        P("dp", None, "sect"),
        P("dp", None, None),
        P("dp", None),
        P(),
        P(),
        P("sect", "dp", None),
        P("sect", "dp", None),
        P("dp", None, None),
    )
    out_specs = (
        P("dp", "sect", None),
        P("dp", "sect", None),
        P("dp", None, "sect"),
        P("dp", None, "sect"),
        P("dp", None, "sect"),
        P("sect", "dp", None),
        P("sect", "dp", None),
        P(),
    )
    return jax.shard_map(
        on_device, mesh=mesh, in_specs=in_specs, out_specs=out_specs, check_vma=False
    )
```

```python
import functools

import jax
import jax.numpy as jnp
from jax import lax
from jax.experimental import pallas as pl
from jax.experimental.pallas import tpu as pltpu
from jax.sharding import PartitionSpec as P

HD = 128
MODALITIES = 3
NZ = 4
NX = 4
NC = 2
NS = 4
AXES = ("dp", "sect")
BF = jnp.bfloat16
F32 = jnp.float32
CAP = 8
VMEM = 20 * 1024 * 1024


def causal_forward(queries, keys, values):
    seq_count, length, width = queries.shape
    head_count = width // HD
    query_f = queries.astype(F32).reshape(seq_count, length, head_count, HD)
    key_f = keys.astype(F32).reshape(seq_count, length, head_count, HD)
    value_f = values.astype(F32).reshape(seq_count, length, head_count, HD)
    scores = jnp.einsum("sqhd,skhd->shqk", query_f, key_f) * HD ** (-0.5)
    position = jnp.arange(length)
    causal = position[:, None] >= position[None, :]
    scores = jnp.where(causal, scores, -1e30)
    probs = jax.nn.softmax(scores, axis=-1)
    probs_b = probs.astype(BF)
    attended = jnp.einsum("shqk,skhd->sqhd", probs_b.astype(F32), value_f)
    return (attended.astype(BF).reshape(seq_count, length, width), probs, probs_b)


def causal_backward(grad_out, queries, keys, values, attended, probs, probs_b):
    seq_count, length, width = queries.shape
    head_count = width // HD
    shape = (seq_count, length, head_count, HD)
    grad_f = grad_out.astype(F32).reshape(shape)
    query_f = queries.astype(F32).reshape(shape)
    key_f = keys.astype(F32).reshape(shape)
    value_f = values.astype(F32).reshape(shape)
    attended_f = attended.astype(F32).reshape(shape)
    value_grad = jnp.einsum("shqk,sqhd->skhd", probs_b.astype(F32), grad_f).astype(BF)
    dprob = jnp.einsum("sqhd,skhd->shqk", grad_f, value_f)
    delta = jnp.einsum("sqhd,sqhd->shq", grad_f, attended_f)
    dscore = (probs * (dprob - delta[..., None]) * HD ** (-0.5)).astype(BF).astype(F32)
    query_grad = jnp.einsum("shqk,skhd->sqhd", dscore, key_f).astype(BF)
    key_grad = jnp.einsum("shqk,sqhd->skhd", dscore, query_f).astype(BF)
    return (
        query_grad.reshape(seq_count, length, width),
        key_grad.reshape(seq_count, length, width),
        value_grad.reshape(seq_count, length, width),
    )


def _pairs(move):
    out = []
    for z in range(NZ):
        for x in range(NX):
            for c in range(NC):
                for s in range(NS):
                    z2, x2, c2, s2 = move(z, x, c, s)
                    source = ((z * NX + x) * NC + c) * NS + s
                    target = (((z2 % NZ) * NX + x2 % NX) * NC + c2) * NS + s2 % NS
                    out.append((source, target))
    return out


def along(first, shift):
    def move(z, x, c, s):
        if (c == 0) == first:
            return z, x + shift, c, s
        return z + shift, x, c, s

    return _pairs(move)


def send(block, pairs):
    return lax.ppermute(block, AXES, pairs)


def send_stage(block, first, shift):
    return send(block, along(first, shift))


def swap_core(block):
    return send(block, _pairs(lambda z, x, c, s: (z, x, 1 - c, s)))


def send_sect(block, shift):
    return send(block, _pairs(lambda z, x, c, s: (z, x, c, s + shift)))


def gather_near(block):
    return jnp.concatenate([block] + [send_stage(block, True, k) for k in (1, 2, 3)], axis=0)


def gather_far(near):
    return [near] + [send_stage(near, False, k) for k in (1, 2, 3)]


def _params(limit=VMEM):
    return pltpu.CompilerParams(vmem_limit_bytes=limit)


def _nt(left, right):
    return lax.dot_general(left, right, (((1,), (1,)), ((), ())), preferred_element_type=F32)


def _slot_selector(labels, kind):
    length = labels.shape[1]
    keep = jnp.broadcast_to((labels == kind).astype(F32), (CAP, length))
    first = lax.broadcasted_iota(jnp.int32, (length, length), 0)
    second = lax.broadcasted_iota(jnp.int32, (length, length), 1)
    rank = jnp.dot(keep, (first <= second).astype(F32), preferred_element_type=F32)
    row = lax.broadcasted_iota(jnp.int32, (CAP, length), 0).astype(F32)
    return jnp.where((rank == row + 1.0) & (keep > 0.5), 1.0, 0.0)


def _slot_spreader(labels, kind):
    length = labels.shape[0]
    keep = jnp.broadcast_to((labels == kind.astype(F32)).astype(F32), (length, CAP))
    first = lax.broadcasted_iota(jnp.int32, (length, length), 0)
    second = lax.broadcasted_iota(jnp.int32, (length, length), 1)
    rank = jnp.dot((second <= first).astype(F32), keep, preferred_element_type=F32)
    column = lax.broadcasted_iota(jnp.int32, (length, CAP), 1).astype(F32)
    return jnp.where((rank == column + 1.0) & (keep > 0.5), 1.0, 0.0)


SMALL_COST = pl.CostEstimate(flops=1000, bytes_accessed=1000, transcendentals=0)
SMALL = pl.BlockSpec(memory_space=pltpu.SMEM)
def _whole(*arrays):
    return [pl.BlockSpec(a.shape, lambda i, n=len(a.shape): (0,) * n) for a in arrays]


RAW = pl.BlockSpec(memory_space=pl.ANY)
FAR = pl.BlockSpec(memory_space=pltpu.HBM)
HELD = pl.BlockSpec(memory_space=pltpu.VMEM)


def _pack_kernel(slot_ref, kinds_hbm, labels_hbm, rows_hbm, out_ref, select_ref, column_ref, *refs):
    kinds_ref, labels_ref, rows_ref, sems = refs
    copies = [
        pltpu.make_async_copy(kinds_hbm, kinds_ref, sems.at[0]),
        pltpu.make_async_copy(labels_hbm, labels_ref, sems.at[1]),
        pltpu.make_async_copy(rows_hbm, rows_ref, sems.at[2]),
    ]
    for copy in copies:
        copy.start()
    copies[0].wait()
    copies[1].wait()
    labels = labels_ref[...]
    length = labels.shape[1]
    select = _slot_selector(labels, kinds_ref[slot_ref[0]]).astype(BF)
    select_ref[...] = select
    first = lax.broadcasted_iota(jnp.int32, (length, length), 0)
    second = lax.broadcasted_iota(jnp.int32, (length, length), 1)
    spread = jnp.where(first == second, jnp.broadcast_to(labels, (length, length)), 0)
    column_ref[...] = jnp.sum(spread.astype(F32), axis=1, keepdims=True)
    copies[2].wait()
    out_ref[...] = jnp.dot(select, rows_ref[...], preferred_element_type=F32).astype(BF)


def pack_rows(slot, kinds, labels, rows):
    length, width = rows.shape
    outs = [
        jax.ShapeDtypeStruct((CAP, width), BF),
        jax.ShapeDtypeStruct((CAP, length), BF),
        jax.ShapeDtypeStruct((length, 1), F32),
    ]
    return pl.pallas_call(
        _pack_kernel,
        in_specs=[SMALL, FAR, FAR, FAR],
        out_specs=[HELD] * 3,
        out_shape=outs,
        scratch_shapes=[
            pltpu.SMEM(kinds.shape, jnp.int32),
            pltpu.VMEM(labels.shape, jnp.int32),
            pltpu.VMEM(rows.shape, BF),
            pltpu.SemaphoreType.DMA((3,)),
        ],
        compiler_params=_params(),
        cost_estimate=SMALL_COST,
    )(slot, kinds, labels, rows)


def _gain_rows(labels, gains):
    return jnp.where(labels == 0.0, gains[0:1], jnp.where(labels == 1.0, gains[1:2], gains[2:3]))


def _norm_kernel(slot_ref, select_ref, column_ref, residual_hbm, gains_hbm, *refs):
    blocks, (hidden_ref, packed_ref, joined_ref, residual_ref, gains_ref, sems) = refs[:NS], refs[NS:]
    copies = [
        pltpu.make_async_copy(residual_hbm, residual_ref, sems.at[0]),
        pltpu.make_async_copy(gains_hbm, gains_ref, sems.at[1]),
    ]
    for copy in copies:
        copy.start()
    slot = slot_ref[0]
    width = blocks[0].shape[1]
    for k, block in enumerate(blocks):
        owner = lax.rem(slot - k + NS, NS)
        joined_ref[:, pl.ds(pl.multiple_of(owner * width, width), width)] = block[...]
    for copy in copies:
        copy.wait()
    hidden = (residual_ref[...].astype(F32) + joined_ref[...].astype(F32)).astype(BF)
    hidden_ref[...] = hidden
    hidden_f = hidden.astype(F32)
    inverse = lax.rsqrt(jnp.mean(hidden_f * hidden_f, axis=-1, keepdims=True) + 1e-05)
    normed = (hidden_f * inverse * _gain_rows(column_ref[...], gains_ref[...])).astype(BF)
    packed_ref[...] = jnp.dot(select_ref[...], normed, preferred_element_type=F32).astype(BF)


def norm_rows_of(slot, select, column, residual, gains, blocks):
    length, width = residual.shape
    outs = [jax.ShapeDtypeStruct((length, width), BF), jax.ShapeDtypeStruct((CAP, width), BF)]
    return pl.pallas_call(
        _norm_kernel,
        in_specs=[SMALL, HELD, HELD, FAR, FAR] + [HELD] * NS,
        out_specs=[HELD, HELD],
        out_shape=outs,
        scratch_shapes=[
            pltpu.VMEM((length, width), BF),
            pltpu.VMEM((length, width), BF),
            pltpu.VMEM(gains.shape, F32),
            pltpu.SemaphoreType.DMA((2,)),
        ],
        compiler_params=_params(),
        cost_estimate=SMALL_COST,
    )(slot, select, column, residual, gains, *blocks)


def _finish_kernel(slot_ref, kinds_ref, column_ref, hidden_ref, cot_ref, gains_ref, *refs):
    sums, (quarter_ref, block_ref, gain_ref, full_ref) = refs[:NS], refs[NS:]
    slot = slot_ref[0]
    labels = column_ref[...]
    kinds = [kinds_ref[lax.rem(slot - k + NS, NS)] for k in range(NS)]
    spreaders = [_slot_spreader(labels, kind) for kind in kinds]
    spread = jnp.concatenate(spreaders, axis=1).astype(BF)
    wide = hidden_ref.shape[1]
    rows = jnp.concatenate([s[:, :wide].astype(F32) for s in sums], axis=0).astype(BF)
    extra = wide // CAP
    parts = [
        s[:, wide : wide + extra].astype(F32) + s[:, wide + extra :].astype(F32) for s in sums
    ]
    for m in range(MODALITIES):
        gain = jnp.zeros_like(parts[0])
        for kind, part in zip(kinds, parts):
            gain = gain + jnp.where(kind == m, part, 0.0)
        gain_ref[m * CAP : (m + 1) * CAP, :] = gain
    norm_grad = jnp.dot(spread, rows, preferred_element_type=F32)
    hidden_f = hidden_ref[...].astype(F32)
    inverse = lax.rsqrt(jnp.mean(hidden_f * hidden_f, axis=-1, keepdims=True) + 1e-05)
    normed_f = hidden_f * inverse
    scaled = norm_grad * _gain_rows(labels, gains_ref[...])
    centre = jnp.mean(scaled * normed_f, axis=-1, keepdims=True)
    full = (cot_ref[...].astype(F32) + inverse * (scaled - normed_f * centre)).astype(BF)
    full_ref[...] = full
    width = block_ref.shape[1]
    block_ref[...] = full_ref[:, pl.ds(pl.multiple_of(slot * width, width), width)]
    wide = full.astype(F32)
    count = quarter_ref.shape[0]
    quarter = wide[:count]
    for t in range(1, NS):
        quarter = jnp.where(slot == t, wide[t * count : (t + 1) * count], quarter)
    quarter_ref[...] = quarter.astype(BF)


def finish_norm(slot, kinds, column, hidden, cot, gains, sums, block_width):
    length, width = hidden.shape
    outs = [
        jax.ShapeDtypeStruct((length // NS, width), BF),
        jax.ShapeDtypeStruct((length, block_width), BF),
        jax.ShapeDtypeStruct((MODALITIES * CAP, width // CAP), F32),
    ]
    return pl.pallas_call(
        _finish_kernel,
        grid=(1,),
        in_specs=[SMALL, SMALL] + _whole(column, hidden, cot, gains, *sums),
        out_specs=_whole(*outs),
        out_shape=outs,
        scratch_shapes=[pltpu.VMEM((length, width), BF)],
        compiler_params=_params(),
        cost_estimate=SMALL_COST,
    )(slot, kinds, column, hidden, cot, gains, *sums)


def _load_kernel(w_hbm, out_ref, sem):
    copy = pltpu.make_async_copy(w_hbm.at[0], out_ref, sem)
    copy.start()
    copy.wait()


def load_weight(weight):
    return pl.pallas_call(
        _load_kernel,
        in_specs=[RAW],
        out_specs=HELD,
        out_shape=pltpu.VMEM(weight.shape[1:], weight.dtype),
        scratch_shapes=[pltpu.SemaphoreType.DMA],
        compiler_params=_params(),
        cost_estimate=SMALL_COST,
    )(weight)


def _back_kernel(*refs):
    pieces, w_ref, out_ref = refs[:8], refs[8], refs[9]
    rows = jnp.concatenate([p[...] for p in pieces], axis=0)
    part = _nt(w_ref[...], rows)

    @pl.when(pl.program_id(0) == 0)
    def _():
        out_ref[...] = part

    @pl.when(pl.program_id(0) > 0)
    def _():
        out_ref[...] += part


def back_product(pieces, weight, tile=4096):
    hidden, width = weight.shape[1:]
    rows = sum(p.shape[0] for p in pieces)
    return pl.pallas_call(
        _back_kernel,
        grid=(width // tile,),
        in_specs=[pl.BlockSpec((p.shape[0], tile), lambda i: (0, i)) for p in pieces]
        + [pl.BlockSpec((None, hidden, tile), lambda i: (0, 0, i))],
        out_specs=pl.BlockSpec((hidden, rows), lambda i: (0, 0)),
        out_shape=jax.ShapeDtypeStruct((hidden, rows), F32),
        compiler_params=_params(),
        cost_estimate=SMALL_COST,
    )(*pieces, weight)


CHUNKS = 2
STEP = 1024
OUT_STEP = 2048


def _pre_kernel(*refs):
    pieces, w_ref, back_ref = refs[:8], refs[8], refs[9]
    act_t_ref, grad_t_ref, act_ref, grad_ref, other_hbm = refs[10:15]
    rows_ref, acc_ref, other_ref, sems, out_sems = refs[15:]
    width = w_ref.shape[1]
    size = width // CHUNKS
    part = pieces[0].shape[0]
    copies = []
    for c in range(CHUNKS):
        span = pl.ds(c * size, size)
        group = []
        for p, piece in enumerate(pieces):
            group.append(
                pltpu.make_async_copy(
                    piece.at[:, span], rows_ref.at[pl.ds(p * part, part), span], sems.at[c, p]
                )
            )
        for copy in group:
            copy.start()
        copies.append(group)
    acc_ref[...] = jnp.zeros_like(acc_ref)
    for c in range(CHUNKS):
        for copy in copies[c]:
            copy.wait()

        @pl.loop(0, size // STEP)
        def _(i):
            span = pl.ds(pl.multiple_of(c * size + i * STEP, STEP), STEP)
            acc_ref[...] += _nt(w_ref[:, span], rows_ref[:, span])

    pre = acc_ref[...]
    sigma = jax.nn.sigmoid(pre)
    act = pre * sigma
    grad = back_ref[...] * sigma * (1.0 + pre * (1.0 - sigma))
    grad_t_ref[...] = grad.astype(BF)
    grad_ref[...] = grad.T.astype(BF)
    half = other_ref.shape[0]
    left = grad_ref[half:, :]
    outs = []
    for n in range(width // OUT_STEP):
        span = pl.ds(n * OUT_STEP, OUT_STEP)
        other_ref[:, span] = jnp.dot(left, w_ref[:, span], preferred_element_type=F32).astype(BF)
        copy = pltpu.make_async_copy(other_ref.at[:, span], other_hbm.at[:, span], out_sems.at[n])
        copy.start()
        outs.append(copy)
    act_t_ref[...] = act.astype(BF)
    act_ref[...] = act.T.astype(BF)
    for copy in outs:
        copy.wait()


def pre_product(pieces, weight, back):
    hidden, width = weight.shape
    rows = sum(p.shape[0] for p in pieces)
    outs = (
        [jax.ShapeDtypeStruct((hidden, rows), BF)] * 2
        + [jax.ShapeDtypeStruct((rows, hidden), BF)] * 2
        + [jax.ShapeDtypeStruct((rows // 2, width), BF)]
    )
    return pl.pallas_call(
        _pre_kernel,
        in_specs=[RAW] * 8 + [HELD, HELD],
        out_specs=[HELD] * 4 + [RAW],
        out_shape=outs,
        scratch_shapes=[
            pltpu.VMEM((rows, width), BF),
            pltpu.VMEM((hidden, rows), F32),
            pltpu.VMEM((rows // 2, width), BF),
            pltpu.SemaphoreType.DMA((CHUNKS, 8)),
            pltpu.SemaphoreType.DMA((width // OUT_STEP,)),
        ],
        compiler_params=_params(),
        cost_estimate=SMALL_COST,
    )(*pieces, weight, back)


def _other_kernel(left_ref, w_ref, out_hbm, out_ref, sems):
    half = out_ref.shape[0]
    left = left_ref[half:, :]
    copies = []
    for n in range(out_ref.shape[1] // OUT_STEP):
        span = pl.ds(n * OUT_STEP, OUT_STEP)
        out_ref[:, span] = jnp.dot(left, w_ref[:, span], preferred_element_type=F32).astype(BF)
        copy = pltpu.make_async_copy(out_ref.at[:, span], out_hbm.at[:, span], sems.at[n])
        copy.start()
        copies.append(copy)
    for copy in copies:
        copy.wait()


def other_product(left, weight):
    width = weight.shape[1]
    half = left.shape[0] // 2
    return pl.pallas_call(
        _other_kernel,
        in_specs=[HELD, HELD],
        out_specs=RAW,
        out_shape=jax.ShapeDtypeStruct((half, width), BF),
        scratch_shapes=[pltpu.VMEM((half, width), BF), pltpu.SemaphoreType.DMA((width // OUT_STEP,))],
        compiler_params=_params(),
        cost_estimate=SMALL_COST,
    )(left, weight)


def _split(value):
    high = value.astype(BF)
    return high, (value - high.astype(F32)).astype(BF)


def _own_kernel(count, left_ref, w_ref, in_ref, *refs):
    rows_hbm, outs = refs[:count], refs[count : count + 4]
    rows_ref, gain_ref, sems = refs[count + 4 :]
    width = w_ref.shape[1]
    half = in_ref.shape[0]
    part = half // 4
    short = width // part
    groups = []
    for n in range(width // OUT_STEP):
        span = pl.ds(n * OUT_STEP, OUT_STEP)
        group = [
            pltpu.make_async_copy(piece.at[:, span], rows_ref.at[pl.ds(p * part, part), span], sems.at[n, p])
            for p, piece in enumerate(rows_hbm)
        ]
        for copy in group:
            copy.start()
        groups.append(group)
    for n, group in enumerate(groups):
        span = pl.ds(n * OUT_STEP, OUT_STEP)
        total = jnp.dot(left_ref[:half, :], w_ref[:, span], preferred_element_type=F32)
        total = total + in_ref[:, span].astype(F32)
        for k, out_ref in enumerate(outs):
            out_ref[:, span] = total[k * part : (k + 1) * part].astype(out_ref.dtype)
        if count:
            for copy in group:
                copy.wait()
            gain = jnp.sum(rows_ref[:, span].astype(F32) * total, axis=0, keepdims=True)
            for j in range(OUT_STEP // short):
                row = n * (OUT_STEP // short) + j
                gain_ref[row : row + 1, :] = gain[:, j * short : (j + 1) * short]
    if count:
        high, low = _split(gain_ref[...])
        outs[0][:, width : width + short] = high.astype(F32) + low.astype(F32)
        outs[0][:, width + short :] = jnp.zeros((part, short), F32)
        for out_ref in outs[1:]:
            out_ref[:, width : width + short] = high
            out_ref[:, width + short :] = low


def own_product(left, weight, arrived, rows=()):
    hidden, width = weight.shape
    half = left.shape[0] // 2
    part = half // 4
    short = width // part
    wide = width + (2 * short if rows else 0)
    kinds = [F32, BF, BF, BF]
    return pl.pallas_call(
        functools.partial(_own_kernel, len(rows)),
        in_specs=[HELD, HELD, HELD] + [RAW] * len(rows),
        out_specs=[HELD] * 4,
        out_shape=[jax.ShapeDtypeStruct((part, wide), kind) for kind in kinds],
        scratch_shapes=[
            pltpu.VMEM((half, width) if rows else (16, 128), BF),
            pltpu.VMEM((part, short), F32),
            pltpu.SemaphoreType.DMA((width // OUT_STEP, max(1, len(rows)))),
        ],
        compiler_params=_params(),
        cost_estimate=SMALL_COST,
    )(left, weight, arrived, *rows)


def _far_norm_kernel(own_ref, *refs):
    arrived, outs = refs[:3], refs[3:]
    part = own_ref.shape[0]
    width = outs[0].shape[1] * CAP // (CAP + 1)
    short = width // part
    total = own_ref[:, :width]
    for ref in arrived:
        total = total + ref[:, :width].astype(F32)
    one, two, three = (
        ref[:, width : width + short].astype(F32) + ref[:, width + short :].astype(F32) for ref in arrived
    )
    gain = (own_ref[:, width : width + short] + two) + (one + three)
    for k, out_ref in enumerate(outs):
        out_ref[:, :width] = total[k * CAP : (k + 1) * CAP]
        for j in range(part // CAP):
            start = width + j * short
            out_ref[:, start : start + short] = gain[j * CAP : (j + 1) * CAP]


def far_norm_sum(pieces, before):
    arrived = [send_stage(pieces[k], False, -k) for k in (1, 2, 3)]
    arrived[0] = after(arrived[0], before)
    part = pieces[0].shape[0]
    width = pieces[0].shape[1] * part // (part + 2)
    outs = [jax.ShapeDtypeStruct((CAP, width + width // CAP), F32)] * 4
    return pl.pallas_call(
        _far_norm_kernel,
        grid=(1,),
        in_specs=_whole(pieces[0], *arrived),
        out_specs=_whole(*outs),
        out_shape=outs,
        compiler_params=_params(),
        cost_estimate=SMALL_COST,
    )(pieces[0], *arrived)


def _near_norm_kernel(*refs):
    zero, one, two, three = (ref[...] for ref in refs[:4])
    out_ref = refs[4]
    width = zero.shape[1] * CAP // (CAP + 1)
    total = (zero + two) + (one + three)
    high, low = _split(total[:, width:])
    out_ref[:, :width] = total[:, :width].astype(BF)
    out_ref[:, width : width + width // CAP] = high
    out_ref[:, width + width // CAP :] = low


def near_norm_sum(blocks, *before):
    arrived = [send_stage(blocks[k], True, -k) for k in (1, 2, 3)]
    arrived[0] = after(arrived[0], *before)
    width = blocks[0].shape[1] * CAP // (CAP + 1)
    out = jax.ShapeDtypeStruct((CAP, width + 2 * (width // CAP)), BF)
    return pl.pallas_call(
        _near_norm_kernel,
        grid=(1,),
        in_specs=_whole(blocks[0], *arrived),
        out_specs=_whole(out)[0],
        out_shape=out,
        compiler_params=_params(),
        cost_estimate=SMALL_COST,
    )(blocks[0], *arrived)


def _near_ffn_kernel(slot_ref, kinds_ref, column_ref, *refs):
    blocks, outs = refs[:4], refs[4:]
    total = blocks[0][...]
    for ref in blocks[1:]:
        total = total + ref[...].astype(F32)
    slot = slot_ref[0]
    spreader = _slot_spreader(column_ref[...], kinds_ref[slot])
    length = spreader.shape[0]
    part = length // NS
    row = lax.broadcasted_iota(jnp.int32, (length, length), 0)
    token = lax.broadcasted_iota(jnp.int32, (length, length), 1)
    turned = jnp.where(token == lax.rem(row + slot * part, length), 1.0, 0.0)
    turned = jnp.dot(turned, spreader, preferred_element_type=F32).astype(BF)
    rows = jnp.dot(turned, total.astype(BF), preferred_element_type=F32)
    for k, out_ref in enumerate(outs):
        out_ref[...] = rows[k * part : (k + 1) * part].astype(BF)


def near_ffn_sum(slot, kinds, column, total, before):
    blocks = [total[k * CAP : (k + 1) * CAP] for k in range(4)]
    arrived = [send_stage(blocks[k].astype(BF), True, -k) for k in (1, 2, 3)]
    arrived[0] = after(arrived[0], before)
    outs = [jax.ShapeDtypeStruct((column.shape[0] // NS, total.shape[1]), BF)] * NS
    return pl.pallas_call(
        _near_ffn_kernel,
        grid=(1,),
        in_specs=[SMALL, SMALL] + _whole(column, blocks[0], *arrived),
        out_specs=_whole(*outs),
        out_shape=outs,
        compiler_params=_params(),
        cost_estimate=SMALL_COST,
    )(slot, kinds, column, blocks[0], *arrived)


def _down_kernel(*refs):
    left_ref, out_ref = refs[8:]
    rows = jnp.concatenate([p[...] for p in refs[:8]], axis=0)
    out_ref[...] = jnp.dot(left_ref[...], rows, preferred_element_type=F32).astype(BF)


def weight_grad(pieces, left, shape, tile=4096):
    _, hidden, width = shape
    count = left.shape[1]
    weight_spec = pl.BlockSpec((None, hidden, tile), lambda i: (0, 0, i))
    return pl.pallas_call(
        _down_kernel,
        grid=(width // tile,),
        in_specs=[pl.BlockSpec((p.shape[0], tile), lambda i: (0, i)) for p in pieces]
        + [pl.BlockSpec((hidden, count), lambda i: (0, 0))],
        out_specs=weight_spec,
        out_shape=jax.ShapeDtypeStruct(shape, BF),
        compiler_params=_params(),
        cost_estimate=pl.CostEstimate(
            flops=2 * hidden * count * width,
            bytes_accessed=2 * width * (hidden + count),
            transcendentals=0,
        ),
    )(*pieces, left)


def after(value, *others):
    return lax.optimization_barrier((value, *others))[0]


def on_device(
    queries, keys, values, residual, labels, slot_modality, gains, up_weight, down_weight, cotangent
):
    slot_index = lax.axis_index("sect")
    slot = slot_index.astype(jnp.int32).reshape(1)
    length = labels.shape[1]
    grad_full = cotangent[0]
    packed_cot, select, column = pack_rows(slot, slot_modality, labels, grad_full)
    queries, keys, values, _ = lax.optimization_barrier((queries, keys, values, packed_cot))
    cot_near = gather_near(packed_cot)

    attended_block, probs, probs_b = causal_forward(queries, keys, values)
    block = attended_block[0]
    blocks = [block] + [send_sect(block, k) for k in (1, 2, 3)]
    hidden, packed = norm_rows_of(slot, after(select, cot_near), column, residual[0], gains, blocks)
    cot_far = gather_far(cot_near)
    cot_rows = cot_far + [swap_core(piece) for piece in cot_far]
    near = gather_near(after(packed, *cot_far[1:]))
    far = gather_far(near)
    back = back_product(cot_rows, down_weight)
    up_held = load_weight(up_weight)
    down_held = load_weight(down_weight)
    far[3] = after(far[3], back, up_held, down_held)
    token_rows = far + [swap_core(piece) for piece in far]

    act_t, grad_t, act, grad, norm_other = pre_product(token_rows, up_held, back)
    norm_arrived = swap_core(norm_other)
    ffn_other = other_product(after(act, norm_other), down_held)
    ffn_arrived = swap_core(ffn_other)
    norm_pieces = own_product(after(grad, ffn_other), up_held, norm_arrived, far)
    ffn_pieces = own_product(after(act, norm_pieces[0]), down_held, ffn_arrived)
    down_grad = weight_grad(cot_rows, after(act_t, ffn_pieces[0]), up_weight.shape)
    norm_blocks = far_norm_sum(norm_pieces, down_grad)
    up_grad = weight_grad(token_rows, after(grad_t, norm_blocks[0]), up_weight.shape)
    ffn_arrived = [send_stage(ffn_pieces[k], False, -k) for k in (1, 2, 3)]
    norm_rows = near_norm_sum(norm_blocks, up_grad, *ffn_arrived)
    ffn_total = after(ffn_pieces[0], norm_rows) + sum(piece.astype(F32) for piece in ffn_arrived)
    sums = [norm_rows] + [send_sect(norm_rows, k) for k in (1, 2, 3)]
    residual_grad, grad_block, gain_part = finish_norm(
        slot, slot_modality, column, hidden, grad_full, gains, sums, queries.shape[2]
    )
    parts = near_ffn_sum(slot, slot_modality, column, ffn_total, grad_block)
    query_grad, key_grad, value_grad = causal_backward(
        after(grad_block, parts[0])[None], queries, keys, values, attended_block, probs, probs_b
    )

    gain_sum = gain_part + swap_core(gain_part)
    width = hidden.shape[1]
    gain_sum = gain_sum.reshape(MODALITIES, CAP, 4, -1).transpose(0, 2, 1, 3).reshape(MODALITIES, width)
    gain_grad = gain_sum / gains

    quarter = length // NS
    total = parts[0].astype(F32)
    for k in (1, 2, 3):
        total = total + send_sect(parts[k], k).astype(F32)
    hidden_q = lax.dynamic_slice_in_dim(hidden, slot_index * quarter, quarter, 0)
    output = (hidden_q.astype(F32) + total).astype(BF)[None]
    return (
        output,
        residual_grad[None],
        query_grad,
        key_grad,
        value_grad,
        up_grad,
        down_grad,
        gain_grad,
    )


def solution(mesh):
    in_specs = (
        P("dp", None, "sect"),
        P("dp", None, "sect"),
        P("dp", None, "sect"),
        P("dp", None, None),
        P("dp", None),
        P(),
        P(),
        P("sect", "dp", None),
        P("sect", "dp", None),
        P("dp", None, None),
    )
    out_specs = (
        P("dp", "sect", None),
        P("dp", "sect", None),
        P("dp", None, "sect"),
        P("dp", None, "sect"),
        P("dp", None, "sect"),
        P("sect", "dp", None),
        P("sect", "dp", None),
        P(),
    )
    return jax.shard_map(
        on_device, mesh=mesh, in_specs=in_specs, out_specs=out_specs, check_vma=False
    )
```
